256 devices in a mesh: gx: 4 (over x), gy: 8 (over y, z_lo), gz: 8 (over z_hi, core).
Axes of the slice: x: 4, y: 4, z: 8 (z_hi: 4, z_lo: 2; z = z_hi * 2 + z_lo), core: 2. Of those that a mesh axis runs over, the one named last changes fastest.
Arguments:
- acts: bfloat16 [2048, 14336], P(('gz', 'gy'), 'gx'), may hold values from -6 to 6
- preact: bfloat16 [2048, 7168], P(('gz', 'gx'), 'gy'), may hold values from -6 to 6
- out_grad: bfloat16 [2048, 14336], P(('gz', 'gy'), 'gx'), may hold values from -2 to 2
- w_in: bfloat16 [14336, 7168], P(('gx', 'gz'), 'gy'), may hold values from -0.046875 to 0.046875
- w_out: bfloat16 [14336, 7168], P(('gx', 'gz'), 'gy'), may hold values from -0.0625 to 0.0625
Outputs:
- input_grad: bfloat16 [2048, 14336], P(('gz', 'gy'), 'gx')
- in_weight_grad: bfloat16 [14336, 7168], P(('gx', 'gz'), 'gy')
- out_weight_grad: bfloat16 [14336, 7168], P(('gx', 'gz'), 'gy')
- bias_grad: float32 [7168], P('gy')
The draws below stay inside these ranges and needn't reach their ends.
All inputs are finite; a program needn't handle non-finite values.
Results may differ from the reference program's by a relative error of at most 0.025.
Values may be sent and summed in bfloat16 or wider, within the bound.
A program may use at most 128 MiB of HBM per device.

```python
import jax
import jax.numpy as jnp
from jax import lax

D = 14336
FF = 7168
ROWS = 256
TOKENS = 2048
N_GY = 8
N_GZ = 8


def steps_of(rng, shape, split, smallest, top_value):
    loudness = 1.0
    for position, blocks in split:
        heights = jax.random.uniform(jax.random.fold_in(jax.random.fold_in(rng, 6), position), (blocks,), jnp.float32, smallest / len(split), top_value / len(split))
        loudness = loudness * jnp.repeat(jnp.exp(heights), shape[position] // blocks).reshape((-1,) + (1,) * (len(shape) - 1 - position))
    return loudness


def bell_draw(own_key, dims, scale, limit, split=(), held_as=jnp.bfloat16):
    level = steps_of(own_key, dims, split, -0.22, 0.18) if split else 1.0
    result = jax.random.normal(own_key, dims, jnp.float32) * scale * level
    return jnp.minimum(jnp.maximum(result, -limit), limit).astype(held_as)


def setup_inputs(seed: int = 0) -> dict:
    key_list = jax.random.split(jax.random.key(seed), 6)
    return {
        "acts": bell_draw(key_list[0], (TOKENS, D), 1.0, 6.0, ((0, 64), (1, 4))),
        "preact": bell_draw(key_list[1], (TOKENS, FF), 1.0, 6.0, ((0, 32), (1, 8))),
        "out_grad": bell_draw(key_list[2], (TOKENS, D), (TOKENS ** -0.25), 2.0, ((0, 64), (1, 4))),
        "w_in": bell_draw(key_list[3], (D, FF), D ** -0.5, 0.046875, ((0, 32), (1, 8))),
        "w_out": bell_draw(key_list[4], (D, FF), FF ** -0.5, 0.0625, ((0, 32), (1, 8))),
    }


def gelu_parts(pre):
    coeff = 0.7978845608028654
    inner = coeff * (pre + 0.044715 * pre * pre * pre)
    tangent = jnp.tanh(inner)
    value = 0.5 * pre * (1.0 + tangent)
    slope = 0.5 * (1.0 + tangent) + 0.5 * pre * (1.0 - tangent * tangent) * coeff * (1.0 + 3.0 * 0.044715 * pre * pre)
    return value, slope


def rounded(term):
    return lax.optimization_barrier(term.astype(jnp.bfloat16)).astype(jnp.float32)


def reference(acts, preact, out_grad, w_in, w_out):
    hidden_grad = jnp.dot(out_grad, w_out, preferred_element_type=jnp.float32)
    value, slope = gelu_parts(preact.astype(jnp.float32))
    act_rounded = value.astype(jnp.bfloat16)
    dh = (hidden_grad * slope).astype(jnp.bfloat16)
    bias_grad = jnp.sum(dh.astype(jnp.float32), axis=0)
    acts_sl = acts.reshape(N_GZ, ROWS, D)
    grad_sl = out_grad.reshape(N_GZ, ROWS, D)
    act_sl = act_rounded.reshape(N_GZ, ROWS, FF)
    dh_sl = dh.reshape(N_GZ, ROWS, FF)

    def depth_step(carry, slices):
        in_acc, out_acc = carry
        x_part, g_part, a_part, d_part = slices
        out_term = jnp.dot(g_part.T, a_part, preferred_element_type=jnp.float32)
        in_term = jnp.dot(x_part.T, d_part, preferred_element_type=jnp.float32)
        return (in_acc + rounded(in_term), out_acc + rounded(out_term)), None

    zeros_w = jnp.zeros((D, FF), jnp.float32)
    (in_total, out_total), _ = lax.scan(depth_step, (zeros_w, zeros_w), (acts_sl, grad_sl, act_sl, dh_sl))
    block = FF // N_GY
    dh_blocks = jnp.transpose(dh.reshape(TOKENS, N_GY, block), (1, 0, 2))
    w_blocks = jnp.transpose(w_in.reshape(D, N_GY, block), (1, 0, 2))

    def hidden_step(carry, blocks):
        d_block, w_block = blocks
        term = jnp.dot(d_block, w_block.T, preferred_element_type=jnp.float32)
        return carry + rounded(term), None

    dx_total, _ = lax.scan(hidden_step, jnp.zeros((TOKENS, D), jnp.float32), (dh_blocks, w_blocks))
    return (dx_total.astype(jnp.bfloat16), in_total.astype(jnp.bfloat16), out_total.astype(jnp.bfloat16), bias_grad)
```

```python
import jax
import jax.numpy as jnp
from jax import lax
from jax.sharding import PartitionSpec as P


def gelu_parts(pre):
    coeff = 0.7978845608028654
    inner = coeff * (pre + 0.044715 * pre * pre * pre)
    tangent = jnp.tanh(inner)
    value = 0.5 * pre * (1.0 + tangent)
    slope = 0.5 * (1.0 + tangent) + 0.5 * pre * (1.0 - tangent * tangent) * coeff * (
        1.0 + 3.0 * 0.044715 * pre * pre
    )
    return (value, slope)


def left_product(left, right):
    return lax.dot_general(
        left, right, (((0,), (0,)), ((), ())), preferred_element_type=jnp.float32
    )


def right_product(left, right):
    return lax.dot_general(
        left, right, (((1,), (1,)), ((), ())), preferred_element_type=jnp.float32
    )


def slice_rows(rows):
    mine = lax.all_to_all(rows, "gz", split_axis=1, concat_axis=0, tiled=True)
    every = lax.all_gather(mine.reshape(8, 1, 32, -1), "gy", axis=1, tiled=True)
    return every.reshape(2048, -1)


def shards(acts, preact, out_grad, w_in, w_out):
    value, slope = gelu_parts(preact.astype(jnp.float32))
    act_rows = lax.all_gather(value.astype(jnp.bfloat16), ("gz", "gx"), axis=0, tiled=True)
    grad_rows = slice_rows(out_grad)
    partial_hidden = jnp.dot(grad_rows, w_out, preferred_element_type=jnp.float32)
    hidden_grad = lax.psum_scatter(
        partial_hidden.astype(jnp.bfloat16), ("gz", "gx"), scatter_dimension=0, tiled=True
    ).astype(jnp.float32)
    acts_rows = slice_rows(acts)
    dh_local = (hidden_grad * slope).astype(jnp.bfloat16)
    dh_rows = lax.all_gather(dh_local, ("gz", "gx"), axis=0, tiled=True)
    partial_input = right_product(dh_rows, w_in).astype(jnp.bfloat16)
    summed = lax.psum_scatter(
        partial_input.reshape(8, 8, 32, -1), "gy", scatter_dimension=1, tiled=True
    )
    input_grad = lax.all_to_all(
        summed.reshape(256, -1), "gz", split_axis=0, concat_axis=1, tiled=True
    )
    bias_grad = jnp.sum(dh_rows.astype(jnp.float32), axis=0)
    out_weight_grad = left_product(grad_rows, act_rows).astype(jnp.bfloat16)
    in_weight_grad = left_product(acts_rows, dh_rows).astype(jnp.bfloat16)
    return (input_grad, in_weight_grad, out_weight_grad, bias_grad)


def solution(mesh):
    return jax.shard_map(
        shards,
        mesh=mesh,
        in_specs=(
            P(("gz", "gy"), "gx"),
            P(("gz", "gx"), "gy"),
            P(("gz", "gy"), "gx"),
            P(("gx", "gz"), "gy"),
            P(("gx", "gz"), "gy"),
        ),
        out_specs=(P(("gz", "gy"), "gx"), P(("gx", "gz"), "gy"), P(("gx", "gz"), "gy"), P("gy")),
        check_vma=False,
    )
```

```python
import jax
import jax.numpy as jnp
from jax import lax
from jax.experimental import pallas as pl
from jax.experimental.pallas import tpu as pltpu
from jax.sharding import PartitionSpec as P

MESH = pl.DeviceIdType.MESH
BF = jnp.bfloat16
F32 = jnp.float32
W = 896
N_SEMS = 160


def gelu_parts(pre):
    coeff = 0.7978845608028654
    inner = coeff * (pre + 0.044715 * pre * pre * pre)
    tangent = jnp.tanh(inner)
    value = 0.5 * pre * (1.0 + tangent)
    slope = 0.5 * (1.0 + tangent) + 0.5 * pre * (1.0 - tangent * tangent) * coeff * (
        1.0 + 3.0 * 0.044715 * pre * pre
    )
    return (value, slope)


def dot(left, right, dims):
    return lax.dot_general(left, right, (dims, ((), ())), preferred_element_type=F32)


class Ring:
    def __init__(self, me, device):
        self.me = me
        self.p, self.m, self.o = (lax.rem(me + k, 4) for k in (1, 3, 2))
        self.plus, self.minus = device(self.p), device(self.m)


def kernel(
    acts, pre, grad, w_in, w_out,
    o_ig, o_iw, o_ow, o_bias,
    G, A, AC, D, WO, WI,
    HP, H1, H2, HX, HS, HB, ZR, SL,
    QP, Q1, Q2, QX, QS, ZS, ZL, IS, IR,
    ACC, OWN, WS, WR, BS, BR,
    send_sem, recv_sem, local_sem,
):
    gx, gy, gz = (lax.axis_index(name) for name in ("gx", "gy", "gz"))
    y, zl = gy // 2, lax.rem(gy, 2)
    zh, core = gz // 2, lax.rem(gz, 2)
    x = gx
    other = 1 - zl

    def dev(x_=x, y_=y, zl_=zl, zh_=zh, c_=core):
        return (x_, y_ * 2 + zl_, zh_ * 2 + c_)

    up, down, opp = (lax.rem(zh + k, 4) for k in (1, 3, 2))
    near = jnp.where(zl == 0, down, up)
    far = jnp.where(zl == 0, up, down)
    order = (zh, near, far, opp)
    twin = dev(c_=1 - core)
    pair = dev(zl_=other)
    rx = Ring(x, lambda k: dev(x_=k))
    ry = Ring(y, lambda k: dev(y_=k))

    peers = [rx.plus, rx.minus, ry.plus, ry.minus, twin, pair]
    peers += [dev(zh_=k) for k in (up, down, opp)]
    peers += [dev(zl_=other, zh_=near), dev(zl_=other, zh_=opp)]
    barrier = pltpu.get_barrier_semaphore()
    for peer in peers:
        pl.semaphore_signal(barrier, inc=1, device_id=peer, device_id_type=MESH)
    pl.semaphore_wait(barrier, len(peers))

    count = [0]
    sends = []

    def sem():
        count[0] += 1
        return count[0] - 1

    def send(k, src, dst, to):
        copy = pltpu.make_async_remote_copy(
            src_ref=src, dst_ref=dst, send_sem=send_sem.at[k], recv_sem=recv_sem.at[k],
            device_id=to, device_id_type=MESH,
        )
        copy.start()
        sends.append(copy)

    def arrived(k, dst):
        pltpu.make_async_remote_copy(
            src_ref=dst, dst_ref=dst, send_sem=send_sem.at[k], recv_sem=recv_sem.at[k],
            device_id=twin, device_id_type=MESH,
        ).wait_recv()

    n_local = [0]

    def local(src, dst):
        copy = pltpu.make_async_copy(src, dst, local_sem.at[n_local[0]])
        n_local[0] += 1
        copy.start()
        return copy

    def half(k):
        return pl.ds(pl.multiple_of(k * 32, 32), 32)

    LO, HI = pl.ds(0, 32), pl.ds(32, 32)

    class Rows:
        def __init__(self, src, buf):
            self.src, self.buf = src, buf
            self.k = [sem() for _ in range(6)]

        def columns(self, k):
            return self.src.at[:, pl.ds(pl.multiple_of(k * W, W), W)]

        def scatter(self):
            k, here = self.k, self.buf.at[zh, y, half(zl)]
            self.own = local(self.columns(zh), here)
            send(k[0], self.columns(zh), here, pair)
            send(k[1], self.columns(far), here, dev(zh_=far))
            send(k[2], self.columns(near), here, dev(zl_=other, zh_=near))
            send(k[3], self.columns(opp), here, dev(zl_=other, zh_=opp))

        def ready(self, t):
            k, buf = self.k, self.buf
            if t == 0:
                self.own.wait()
                arrived(k[0], buf.at[zh, y, half(other)])
            elif t == 1:
                arrived(k[1], buf.at[near, y, half(zl)])
                arrived(k[2], buf.at[near, y, half(other)])
                send(k[4], buf.at[near, y], buf.at[near, y], pair)
            elif t == 2:
                arrived(k[4], buf.at[far, y])
            else:
                piece = buf.at[opp, y, half(other)]
                arrived(k[3], piece)
                send(k[5], piece, piece, pair)
                arrived(k[5], buf.at[opp, y, half(zl)])

    class Gather:
        def __init__(self, buf, ring, s):
            self.buf, self.ring, self.s = buf, ring, s
            self.k = [sem() for _ in range(4)]

        def at(self, block, rows=pl.ds(0, 64)):
            return self.buf.at[self.s, block, rows]

        def start(self):
            r, mine = self.ring, self.at(self.ring.me)
            send(self.k[0], mine, mine, r.plus)
            send(self.k[1], mine, mine, r.minus)

        def forward(self):
            r = self.ring
            arrived(self.k[0], self.at(r.m))
            send(self.k[2], self.at(r.m, LO), self.at(r.m, LO), r.plus)
            arrived(self.k[1], self.at(r.p))
            send(self.k[3], self.at(r.p, HI), self.at(r.p, HI), r.minus)

        def done(self):
            r = self.ring
            arrived(self.k[2], self.at(r.o, LO))
            arrived(self.k[3], self.at(r.o, HI))

    class Scatter:
        def __init__(self, part, first, second, mixed, ring, t):
            self.part, self.first, self.second, self.mixed = (
                part.at[t], first.at[t], second.at[t], mixed.at[t]
            )
            self.ring = ring
            self.k = [sem() for _ in range(6)]

        def start(self):
            r, k = self.ring, self.k
            send(k[0], self.part.at[r.o, LO], self.first.at[0], r.plus)
            send(k[1], self.part.at[r.o, HI], self.first.at[1], r.minus)
            send(k[2], self.part.at[r.p, HI], self.second.at[0, HI], r.plus)
            send(k[3], self.part.at[r.m, LO], self.second.at[1, LO], r.minus)

        def middle(self):
            r, k = self.ring, self.k
            for way, rows, block, to in ((0, LO, r.p, r.plus), (1, HI, r.m, r.minus)):
                arrived(k[way], self.first.at[way])
                total = self.part[block, rows].astype(F32) + self.first[way].astype(F32)
                self.mixed[way] = total.astype(BF)
                send(k[4 + way], self.mixed.at[way], self.second.at[way, rows], to)

        def end(self):
            k = self.k
            arrived(k[2], self.second.at[0, HI])
            arrived(k[3], self.second.at[1, LO])
            arrived(k[4], self.second.at[0, LO])
            arrived(k[5], self.second.at[1, HI])
            return (
                self.part[self.ring.me].astype(F32)
                + self.second[0].astype(F32)
                + self.second[1].astype(F32)
            )

    class Depth:
        def __init__(self, buf):
            self.buf = buf
            self.k = [sem() for _ in range(3)]

        def start(self):
            mine = self.buf.at[zh, x]
            for k, to in zip(self.k, (near, far, opp)):
                send(k, mine, mine, dev(zh_=to))

        def ready(self, t):
            k = self.k[(None, 1, 0, 2)[t]]
            arrived(k, self.buf.at[order[t], x])

    rows_g, rows_a = Rows(grad, G), Rows(acts, A)
    g_y = [Gather(G, ry, s) for s in order]
    a_y = Gather(A, ry, pl.ds(0, 4))
    c_z, c_x = Depth(AC), Gather(AC, rx, pl.ds(0, 4))
    h_x = [Scatter(HP, H1, H2, HX, rx, t) for t in range(4)]
    h_k = [sem() for _ in range(3)]
    d_z, d_x = Depth(D), [Gather(D, rx, s) for s in order]
    q_y = [Scatter(QP, Q1, Q2, QX, ry, t) for t in range(4)]
    q_k = [sem() for _ in range(4)]
    i_k = [sem() for _ in range(3)]
    w_k = [sem() for _ in range(2)]
    g_k = [sem() for _ in range(2)]
    b_k = sem()

    mine = pl.ds(pl.multiple_of(core * 448, 448), 448)
    theirs = pl.ds(pl.multiple_of((1 - core) * 448, 448), 448)

    rows_g.scatter()
    own_w = []
    for k, src, buf in ((w_k[0], w_out, WO), (w_k[1], w_in, WI)):
        send(k, src, buf.at[mine], twin)
        own_w.append(local(src, buf.at[mine]))

    value, slope = gelu_parts(pre[...].astype(F32))
    AC[zh, x] = value.astype(BF)
    SL[...] = slope

    def hidden(t):
        g_y[t].done()
        if t == 0:
            own_w[0].wait()
            arrived(w_k[0], WO.at[theirs])
        part = dot(G[order[t]].reshape(256, W), WO[...], ((1,), (0,)))
        HP[t] = part.astype(BF).reshape(4, 64, W)
        h_x[t].start()

    def hidden_end(t):
        total = h_x[t].end()
        if t == 0:
            HS[3] = total
        else:
            HB[t - 1] = total.astype(BF)
            send(h_k[t - 1], HB.at[t - 1], ZR.at[t - 1], dev(zh_=order[t]))

    rows_g.ready(0)
    g_y[0].start()
    rows_g.ready(1)
    g_y[1].start()
    g_y[0].forward()
    rows_g.ready(2)
    g_y[2].start()
    g_y[1].forward()
    rows_g.ready(3)
    g_y[3].start()
    c_z.start()
    rows_a.scatter()
    hidden(0)
    g_y[2].forward()
    hidden(1)
    h_x[0].middle()
    g_y[3].forward()
    hidden(2)
    h_x[1].middle()
    hidden_end(0)
    for t in range(4):
        rows_a.ready(t)
    a_y.start()
    hidden(3)
    h_x[2].middle()
    hidden_end(1)
    h_x[3].middle()
    for t in range(1, 4):
        c_z.ready(t)
    c_x.start()
    hidden_end(2)
    hidden_end(3)
    a_y.forward()

    total = HS[3]
    for t in range(3):
        arrived(h_k[t], ZR.at[t])
        total = total + ZR[t].astype(F32)
    D[zh, x] = (total * SL[...]).astype(BF)
    d_x[0].start()
    d_z.start()

    def weight_grad(rows, cols, t, first):
        right = cols[order[t]].reshape(256, W)

        def step(i, carry):
            at = pl.ds(pl.multiple_of(i * 128, 128), 128)
            left = rows[order[t], :, :, at].reshape(256, 128)
            term = dot(left, right, ((0,), (0,)))
            if first:
                ACC[at] = term
            else:
                ACC[at] += term
            return carry

        lax.fori_loop(0, 7, step, 0)

    def share(i):
        WS[i] = ACC[theirs].astype(BF)
        send(g_k[i], WS.at[i], WR.at[i], twin)
        OWN[i] = ACC[mine]

    def inputs(t):
        d_x[t].done()
        if t == 0:
            own_w[1].wait()
            arrived(w_k[1], WI.at[theirs])
        part = dot(D[order[t]].reshape(256, W), WI[...], ((1,), (1,)))
        QP[t] = part.astype(BF).reshape(4, 64, W)
        q_y[t].start()

    def inputs_end(t):
        QS[t] = q_y[t].end()
        ZS[t] = QS[t, half(other)].astype(BF)
        there = (0, 2, 1, 3)[t]
        send(q_k[there], ZS.at[t], ZL.at[there], pair)

    def inputs_out(t):
        arrived(q_k[t], ZL.at[t])
        total = (QS[t, half(zl)] + ZL[t].astype(F32)).astype(BF)
        if t == 0:
            IR[zh] = total
        else:
            IS[t] = total
            send(i_k[t - 1], IS.at[t], IR.at[zh], dev(zh_=order[t]))

    d_z.ready(1)
    d_x[1].start()
    d_x[0].forward()
    d_z.ready(2)
    d_x[2].start()
    d_x[1].forward()
    d_z.ready(3)
    d_x[3].start()
    inputs(0)
    d_x[2].forward()
    inputs(1)
    q_y[0].middle()
    d_x[3].forward()
    c_x.forward()
    a_y.done()
    weight_grad(A, D, 0, True)
    inputs(2)
    q_y[1].middle()
    inputs_end(0)
    weight_grad(A, D, 1, False)
    inputs(3)
    q_y[2].middle()
    inputs_end(1)
    inputs_out(0)
    weight_grad(A, D, 2, False)
    q_y[3].middle()
    inputs_end(2)
    inputs_out(1)
    weight_grad(A, D, 3, False)
    share(0)
    inputs_end(3)
    inputs_out(2)
    sums = jnp.sum(D[...].astype(F32).reshape(128, 8, W), axis=0)
    BS[...] = sums
    send(b_k, BS, BR, twin)
    inputs_out(3)
    c_x.done()
    for t in range(4):
        weight_grad(G, AC, t, t == 0)
    share(1)

    for t in range(1, 4):
        arrived(i_k[(None, 1, 0, 2)[t] ], IR.at[order[t]])
    for k in range(4):
        o_ig[:, k * W : (k + 1) * W] = IR[k]
    arrived(b_k, BR)
    o_bias[...] = jnp.sum(BS[...] + BR[...], axis=0, keepdims=True)
    for i, out in ((0, o_iw), (1, o_ow)):
        arrived(g_k[i], WR.at[i])
        out[...] = (OWN[i] + WR[i].astype(F32)).astype(BF)
    for copy in sends:
        copy.wait_send()


def shards(acts, preact, out_grad, w_in, w_out):
    vmem = pl.BlockSpec(memory_space=pltpu.VMEM)
    bf = lambda *shape: pltpu.VMEM(shape, BF)
    f32 = lambda *shape: pltpu.VMEM(shape, F32)
    scratch = dict(
        G=bf(4, 4, 64, W), A=bf(4, 4, 64, W), AC=bf(4, 4, 64, W), D=bf(4, 4, 64, W),
        WO=bf(W, W), WI=bf(W, W),
        HP=bf(4, 4, 64, W), H1=bf(4, 2, 32, W), H2=bf(4, 2, 64, W), HX=bf(4, 2, 32, W),
        HS=f32(4, 64, W), HB=bf(3, 64, W), ZR=bf(3, 64, W), SL=f32(64, W),
        QP=bf(4, 4, 64, W), Q1=bf(4, 2, 32, W), Q2=bf(4, 2, 64, W), QX=bf(4, 2, 32, W),
        QS=f32(4, 64, W), ZS=bf(4, 32, W), ZL=bf(4, 32, W), IS=bf(4, 32, W), IR=bf(4, 32, W),
        ACC=f32(W, W), OWN=f32(2, 448, W), WS=bf(2, 448, W), WR=bf(2, 448, W),
        BS=f32(8, W), BR=f32(8, W),
        send_sem=pltpu.SemaphoreType.DMA((N_SEMS,)),
        recv_sem=pltpu.SemaphoreType.DMA((N_SEMS,)),
        local_sem=pltpu.SemaphoreType.DMA((8,)),
    )
    input_grad, in_weight_grad, out_weight_grad, bias_grad = pl.pallas_call(
        kernel,
        out_shape=(
            jax.ShapeDtypeStruct((32, 4 * W), BF),
            jax.ShapeDtypeStruct((448, W), BF),
            jax.ShapeDtypeStruct((448, W), BF),
            jax.ShapeDtypeStruct((1, W), F32),
        ),
        in_specs=[vmem] * 5,
        out_specs=[vmem] * 4,
        scratch_shapes=list(scratch.values()),
        compiler_params=pltpu.CompilerParams(
            collective_id=0, has_side_effects=True, vmem_limit_bytes=60 * 2**20
        ),
    )(acts, preact, out_grad, w_in, w_out)
    return (input_grad, in_weight_grad, out_weight_grad, bias_grad.reshape(W))


def solution(mesh):
    return jax.shard_map(
        shards,
        mesh=mesh,
        in_specs=(
            P(("gz", "gy"), "gx"),
            P(("gz", "gx"), "gy"),
            P(("gz", "gy"), "gx"),
            P(("gx", "gz"), "gy"),
            P(("gx", "gz"), "gy"),
        ),
        out_specs=(P(("gz", "gy"), "gx"), P(("gx", "gz"), "gy"), P(("gx", "gz"), "gy"), P("gy")),
        check_vma=False,
    )
```

```python
import jax
import jax.numpy as jnp
from jax import lax
from jax.experimental import pallas as pl
from jax.experimental.pallas import tpu as pltpu
from jax.sharding import PartitionSpec as P

MESH = pl.DeviceIdType.MESH
BF = jnp.bfloat16
F32 = jnp.float32
W = 896
N_SEMS = 160


def gelu_parts(pre):
    coeff = 0.7978845608028654
    inner = coeff * (pre + 0.044715 * pre * pre * pre)
    tangent = jnp.tanh(inner)
    value = 0.5 * pre * (1.0 + tangent)
    slope = 0.5 * (1.0 + tangent) + 0.5 * pre * (1.0 - tangent * tangent) * coeff * (
        1.0 + 3.0 * 0.044715 * pre * pre
    )
    return (value, slope)


def dot(left, right, dims):
    return lax.dot_general(left, right, (dims, ((), ())), preferred_element_type=F32)


class Ring:
    def __init__(self, me, device):
        self.me = me
        self.p, self.m, self.o = (lax.rem(me + k, 4) for k in (1, 3, 2))
        self.plus, self.minus = device(self.p), device(self.m)


def kernel(
    acts_hbm, pre_hbm, grad_hbm, w_in, w_out,
    o_ig, o_iw, o_ow, o_bias,
    acts, pre, grad, OUT,
    G, A, AC, D, WO, WI,
    HP, H1, H2, HX, HS, HB, ZR, SL,
    QP, Q1, Q2, QX, QS, ZS, ZL, IS, IR,
    ACC, WS, WR, BS, BR,
    send_sem, recv_sem, local_sem,
):
    gx, gy, gz = (lax.axis_index(name) for name in ("gx", "gy", "gz"))
    y, zl = gy // 2, lax.rem(gy, 2)
    zh, core = gz // 2, lax.rem(gz, 2)
    x = gx
    other = 1 - zl

    def dev(x_=x, y_=y, zl_=zl, zh_=zh, c_=core):
        return (x_, y_ * 2 + zl_, zh_ * 2 + c_)

    up, down, opp = (lax.rem(zh + k, 4) for k in (1, 3, 2))
    near = jnp.where(zl == 0, down, up)
    far = jnp.where(zl == 0, up, down)
    order = (zh, near, far, opp)
    ring = (zh, up, down, opp)
    twin = dev(c_=1 - core)
    pair = dev(zl_=other)
    rx = Ring(x, lambda k: dev(x_=k))
    ry = Ring(y, lambda k: dev(y_=k))

    peers = [rx.plus, rx.minus, ry.plus, ry.minus, twin, pair]
    peers += [dev(zh_=k) for k in (up, down, opp)]
    peers += [dev(zl_=other, zh_=near), dev(zl_=other, zh_=opp)]
    barrier = pltpu.get_barrier_semaphore()
    for peer in peers:
        pl.semaphore_signal(barrier, inc=1, device_id=peer, device_id_type=MESH)

    count = [0]
    sends = []

    def sem():
        count[0] += 1
        return count[0] - 1

    def send(k, src, dst, to):
        copy = pltpu.make_async_remote_copy(
            src_ref=src, dst_ref=dst, send_sem=send_sem.at[k], recv_sem=recv_sem.at[k],
            device_id=to, device_id_type=MESH,
        )
        copy.start()
        sends.append(copy)

    def arrived(k, dst):
        pltpu.make_async_remote_copy(
            src_ref=dst, dst_ref=dst, send_sem=send_sem.at[k], recv_sem=recv_sem.at[k],
            device_id=twin, device_id_type=MESH,
        ).wait_recv()

    n_local = [0]

    def local(src, dst):
        copy = pltpu.make_async_copy(src, dst, local_sem.at[n_local[0]])
        n_local[0] += 1
        copy.start()
        return copy

    staged = [local(a, b) for a, b in ((grad_hbm, grad), (pre_hbm, pre), (acts_hbm, acts))]

    def half(k):
        return pl.ds(pl.multiple_of(k * 32, 32), 32)

    LO, HI = pl.ds(0, 32), pl.ds(32, 32)

    class Rows:
        def __init__(self, src, buf):
            self.src, self.buf = src, buf
            self.k = [sem() for _ in range(6)]

        def columns(self, k):
            return self.src.at[:, pl.ds(pl.multiple_of(k * W, W), W)]

        def scatter(self):
            k, here = self.k, self.buf.at[zh, y, half(zl)]
            send(k[1], self.columns(far), here, dev(zh_=far))
            send(k[2], self.columns(near), here, dev(zl_=other, zh_=near))
            send(k[3], self.columns(opp), here, dev(zl_=other, zh_=opp))
            send(k[0], self.columns(zh), here, pair)
            self.own = local(self.columns(zh), here)

        def own_ready(self):
            self.own.wait()
            arrived(self.k[0], self.buf.at[zh, y, half(other)])

        def near_ready(self):
            block = self.buf.at[near, y]
            arrived(self.k[1], self.buf.at[near, y, half(zl)])
            arrived(self.k[2], self.buf.at[near, y, half(other)])
            send(self.k[4], block, block, pair)

        def far_ready(self):
            arrived(self.k[4], self.buf.at[far, y])

        def opp_half(self):
            piece = self.buf.at[opp, y, half(other)]
            arrived(self.k[3], piece)
            send(self.k[5], piece, piece, pair)

        def opp_ready(self):
            arrived(self.k[5], self.buf.at[opp, y, half(zl)])

    class Gather:
        def __init__(self, buf, ring, s):
            self.buf, self.ring, self.s = buf, ring, s
            self.k = [sem() for _ in range(4)]

        def at(self, block, rows=pl.ds(0, 64)):
            return self.buf.at[self.s, block, rows]

        def start(self):
            r, mine = self.ring, self.at(self.ring.me)
            send(self.k[0], mine, mine, r.plus)
            send(self.k[1], mine, mine, r.minus)

        def forward(self):
            r = self.ring
            arrived(self.k[0], self.at(r.m))
            send(self.k[2], self.at(r.m, LO), self.at(r.m, LO), r.plus)
            arrived(self.k[1], self.at(r.p))
            send(self.k[3], self.at(r.p, HI), self.at(r.p, HI), r.minus)

        def done(self):
            r = self.ring
            arrived(self.k[2], self.at(r.o, LO))
            arrived(self.k[3], self.at(r.o, HI))

    class Scatter:
        def __init__(self, part, first, second, mixed, ring, t):
            self.part, self.first, self.second, self.mixed = (
                part.at[t], first.at[t], second.at[t], mixed.at[t]
            )
            self.ring = ring
            self.k = [sem() for _ in range(6)]

        def start(self):
            r, k = self.ring, self.k
            send(k[0], self.part.at[r.o, LO], self.first.at[0], r.plus)
            send(k[1], self.part.at[r.o, HI], self.first.at[1], r.minus)
            send(k[2], self.part.at[r.p, HI], self.second.at[0, HI], r.plus)
            send(k[3], self.part.at[r.m, LO], self.second.at[1, LO], r.minus)

        def middle(self):
            r, k = self.ring, self.k
            for way, rows, block, to in ((0, LO, r.p, r.plus), (1, HI, r.m, r.minus)):
                arrived(k[way], self.first.at[way])
                total = self.part[block, rows].astype(F32) + self.first[way].astype(F32)
                self.mixed[way] = total.astype(BF)
                send(k[4 + way], self.mixed.at[way], self.second.at[way, rows], to)

        def end(self):
            k = self.k
            arrived(k[2], self.second.at[0, HI])
            arrived(k[3], self.second.at[1, LO])
            arrived(k[4], self.second.at[0, LO])
            arrived(k[5], self.second.at[1, HI])
            return (
                self.part[self.ring.me].astype(F32)
                + self.second[0].astype(F32)
                + self.second[1].astype(F32)
            )

    class Depth:
        def __init__(self, buf):
            self.buf = buf
            self.k = [sem() for _ in range(4)]

        def start(self):
            mine = self.buf.at[zh, x]
            send(self.k[0], mine, mine, dev(zh_=up))
            send(self.k[1], mine, mine, dev(zh_=down))

        def forward(self):
            for k, came, rows, to in ((0, down, LO, up), (1, up, HI, down)):
                arrived(self.k[k], self.buf.at[came, x])
                piece = self.buf.at[came, x, rows]
                send(self.k[k + 2], piece, piece, dev(zh_=to))

        def done(self):
            arrived(self.k[2], self.buf.at[opp, x, LO])
            arrived(self.k[3], self.buf.at[opp, x, HI])

    rows_g, rows_a = Rows(grad, G), Rows(acts, A)
    g_y = [Gather(G, ry, s) for s in order]
    a_y = [Gather(A, ry, s) for s in order]
    c_z, c_x = Depth(AC), [Gather(AC, rx, s) for s in order]
    h_x = [Scatter(HP, H1, H2, HX, rx, t) for t in range(4)]
    h_k = [sem() for _ in range(3)]
    d_z, d_x = Depth(D), [Gather(D, rx, s) for s in ring]
    q_y = [Scatter(QP, Q1, Q2, QX, ry, t) for t in range(4)]
    q_k = [sem() for _ in range(4)]
    i_k = [sem() for _ in range(3)]
    w_k = [sem() for _ in range(2)]
    g_k = [sem() for _ in range(2)]
    b_k = sem()
    OWN, NEAR, FAR, OPP = range(4)
    UP, DOWN = 1, 2

    mine = pl.ds(pl.multiple_of(core * 448, 448), 448)
    theirs = pl.ds(pl.multiple_of((1 - core) * 448, 448), 448)
    own_w = [None, None]
    results = []

    def weights(i, src, buf):
        send(w_k[i], src, buf.at[mine], twin)
        own_w[i] = local(src, buf.at[mine])

    def activations():
        staged[1].wait()
        value, slope = gelu_parts(pre[...].astype(F32))
        AC[zh, x] = value.astype(BF)
        SL[...] = slope

    def entry():
        pl.semaphore_wait(barrier, len(peers))
        staged[0].wait()

    def hidden(t, first=False):
        g_y[t].done()
        if first:
            own_w[0].wait()
            arrived(w_k[0], WO.at[theirs])
        part = dot(G[order[t]].reshape(256, W), WO[...], ((1,), (0,)))
        HP[t] = part.astype(BF).reshape(4, 64, W)
        h_x[t].start()

    def hidden_end(t):
        total = h_x[t].end()
        if t == OWN:
            HS[...] = total
        else:
            HB[t - 1] = total.astype(BF)
            send(h_k[t - 1], HB.at[t - 1], ZR.at[t - 1], dev(zh_=order[t]))

    def dh_rows():
        total = HS[...]
        for t in range(3):
            arrived(h_k[t], ZR.at[t])
            total = total + ZR[t].astype(F32)
        D[zh, x] = (total * SL[...]).astype(BF)

    def weight_grad(i, t, first=False):
        rows, cols = ((A, D), (G, AC))[i]
        s = ring[t] if i == 0 else order[t]
        right = cols[s].reshape(256, W)
        for low, size in ((0, 512), (512, 384)):
            left = rows[s, :, :, low : low + size].reshape(256, size)
            term = dot(left, right, ((0,), (0,)))
            if first:
                ACC[i, low : low + size] = term
            else:
                ACC[i, low : low + size] += term

    def share(i):
        WS[i] = ACC[i, theirs].astype(BF)
        send(g_k[i], WS.at[i], WR.at[i], twin)

    def inputs(t, first=False):
        d_x[t].done()
        if first:
            own_w[1].wait()
            arrived(w_k[1], WI.at[theirs])
        part = dot(D[ring[t]].reshape(256, W), WI[...], ((1,), (1,)))
        QP[t] = part.astype(BF).reshape(4, 64, W)
        q_y[t].start()

    def inputs_end(t):
        QS[t] = q_y[t].end()
        ZS[t] = QS[t, half(other)].astype(BF)
        send(q_k[t], ZS.at[t], ZL.at[t], pair)

    def inputs_out(t):
        arrived(q_k[t], ZL.at[t])
        total = (QS[t, half(zl)] + ZL[t].astype(F32)).astype(BF)
        if t == OWN:
            IR[zh] = total
        else:
            IS[t] = total
            send(i_k[t - 1], IS.at[t], IR.at[zh], dev(zh_=ring[t]))

    def bias_sums():
        BS[...] = jnp.sum(D[...].astype(F32).reshape(128, 8, W), axis=0)
        send(b_k, BS, BR, twin)

    def finish_bias():
        arrived(b_k, BR)
        o_bias[...] = jnp.sum(BS[...] + BR[...], axis=0, keepdims=True)

    def finish_weight(i, out):
        arrived(g_k[i], WR.at[i])
        OUT[i] = (ACC[i, mine] + WR[i].astype(F32)).astype(BF)
        results.append(local(OUT.at[i], out))

    def finish_inputs():
        for t in range(1, 4):
            arrived(i_k[(None, 1, 0, 2)[t]], IR.at[ring[t]])
        for k in range(4):
            results.append(local(IR.at[k], o_ig.at[:, pl.ds(k * W, W)]))

    def finish_sends():
        for copy in sends:
            copy.wait_send()
        for copy in results:
            copy.wait()

    activations()
    entry()
    rows_g.scatter()
    weights(0, w_out, WO)
    c_x[OWN].start()
    rows_g.near_ready()
    g_y[NEAR].start()
    rows_g.far_ready()
    g_y[FAR].start()
    rows_g.opp_half()
    g_y[NEAR].forward()
    rows_g.opp_ready()
    g_y[OPP].start()
    weights(1, w_in, WI)
    c_x[OWN].forward()
    g_y[FAR].forward()
    hidden(NEAR, True)
    rows_g.own_ready()
    g_y[OWN].start()
    g_y[OPP].forward()
    staged[2].wait()
    rows_a.scatter()
    h_x[NEAR].middle()
    hidden(FAR)
    g_y[OWN].forward()
    hidden_end(NEAR)
    h_x[FAR].middle()
    c_z.start()
    hidden(OPP)
    rows_a.near_ready()
    rows_a.opp_half()
    hidden_end(FAR)
    h_x[OPP].middle()
    rows_a.far_ready()
    a_y[NEAR].start()
    a_y[FAR].start()
    hidden(OWN)
    hidden_end(OPP)
    h_x[OWN].middle()
    rows_a.opp_ready()
    a_y[NEAR].forward()
    a_y[OPP].start()
    rows_a.own_ready()
    a_y[FAR].forward()
    a_y[OWN].start()
    hidden_end(OWN)
    c_z.forward()
    c_x[NEAR].start()
    c_x[OWN].done()
    weight_grad(1, OWN, True)
    dh_rows()
    d_x[OWN].start()
    d_z.start()
    c_x[NEAR].forward()
    a_y[OPP].forward()
    d_x[OWN].forward()
    a_y[OWN].forward()
    d_z.forward()
    d_x[UP].start()
    d_x[DOWN].start()
    inputs(OWN, True)
    q_y[OWN].middle()
    d_x[UP].forward()
    d_z.done()
    d_x[OPP].start()
    inputs_end(OWN)
    d_x[DOWN].forward()
    inputs(UP)
    inputs_out(OWN)
    c_x[FAR].start()
    q_y[UP].middle()
    for t in range(4):
        a_y[t].done()
    weight_grad(0, OWN, True)
    d_x[OPP].forward()
    inputs(DOWN)
    inputs_end(UP)
    q_y[DOWN].middle()
    c_x[FAR].forward()
    c_z.done()
    c_x[OPP].start()
    weight_grad(0, UP)
    inputs(OPP)
    inputs_end(DOWN)
    weight_grad(0, DOWN)
    inputs_out(UP)
    weight_grad(0, OPP)
    share(0)
    q_y[OPP].middle()
    inputs_out(DOWN)
    c_x[OPP].forward()
    c_x[NEAR].done()
    weight_grad(1, NEAR)
    c_x[FAR].done()
    weight_grad(1, FAR)
    inputs_end(OPP)
    bias_sums()
    finish_weight(0, o_iw)
    inputs_out(OPP)
    c_x[OPP].done()
    weight_grad(1, OPP)
    share(1)
    finish_bias()
    finish_inputs()
    finish_weight(1, o_ow)
    finish_sends()


def deliver(from_ig, from_iw, from_ow, from_bias, o_ig, o_iw, o_ow, o_bias, h_ig, h_iw, h_ow, get, put):
    pieces = []
    for src, held, dst, rows in (
        (from_iw, h_iw, o_iw, 224), (from_ow, h_ow, o_ow, 224), (from_ig, h_ig, o_ig, 32)
    ):
        for k in range(src.shape[0] // rows):
            at = pl.ds(k * rows, rows)
            pieces.append((src.at[at], held.at[at], dst.at[at]))
    ins = [pltpu.make_async_copy(a, b, get.at[k]) for k, (a, b, _) in enumerate(pieces)]
    outs = [pltpu.make_async_copy(b, c, put.at[k]) for k, (_, b, c) in enumerate(pieces)]
    for copy in ins:
        copy.start()
    o_bias[...] = from_bias[0]
    for came, go in zip(ins, outs):
        came.wait()
        go.start()
    for copy in outs:
        copy.wait()


def shards(acts, preact, out_grad, w_in, w_out):
    vmem = pl.BlockSpec(memory_space=pltpu.VMEM)
    bf = lambda *shape: pltpu.VMEM(shape, BF)
    f32 = lambda *shape: pltpu.VMEM(shape, F32)
    scratch = dict(
        acts=bf(32, 4 * W), pre=bf(64, W), grad=bf(32, 4 * W), OUT=bf(2, 448, W),
        G=bf(4, 4, 64, W), A=bf(4, 4, 64, W), AC=bf(4, 4, 64, W), D=bf(4, 4, 64, W),
        WO=bf(W, W), WI=bf(W, W),
        HP=bf(4, 4, 64, W), H1=bf(4, 2, 32, W), H2=bf(4, 2, 64, W), HX=bf(4, 2, 32, W),
        HS=f32(64, W), HB=bf(3, 64, W), ZR=bf(3, 64, W), SL=f32(64, W),
        QP=bf(4, 4, 64, W), Q1=bf(4, 2, 32, W), Q2=bf(4, 2, 64, W), QX=bf(4, 2, 32, W),
        QS=f32(4, 64, W), ZS=bf(4, 32, W), ZL=bf(4, 32, W), IS=bf(4, 32, W), IR=bf(4, 32, W),
        ACC=f32(2, W, W), WS=bf(2, 448, W), WR=bf(2, 448, W),
        BS=f32(8, W), BR=f32(8, W),
        send_sem=pltpu.SemaphoreType.DMA((N_SEMS,)),
        recv_sem=pltpu.SemaphoreType.DMA((N_SEMS,)),
        local_sem=pltpu.SemaphoreType.DMA((16,)),
    )
    hbm = pl.BlockSpec(memory_space=pl.ANY)
    parts = pl.pallas_call(
        kernel,
        out_shape=(
            jax.ShapeDtypeStruct((32, 4 * W), BF),
            jax.ShapeDtypeStruct((448, W), BF),
            jax.ShapeDtypeStruct((448, W), BF),
            jax.ShapeDtypeStruct((1, W), F32),
        ),
        in_specs=[hbm] * 5,
        out_specs=[hbm] * 3 + [vmem],
        scratch_shapes=list(scratch.values()),
        compiler_params=pltpu.CompilerParams(
            collective_id=0, has_side_effects=True, vmem_limit_bytes=60 * 2**20
        ),
    )(acts, preact, out_grad, w_in, w_out)
    return tuple(
        pl.pallas_call(
            deliver,
            out_shape=(
                jax.ShapeDtypeStruct((32, 4 * W), BF),
                jax.ShapeDtypeStruct((448, W), BF),
                jax.ShapeDtypeStruct((448, W), BF),
                jax.ShapeDtypeStruct((W,), F32),
            ),
            in_specs=[hbm] * 3 + [vmem],
            out_specs=[hbm] * 3 + [vmem],
            scratch_shapes=[
                bf(32, 4 * W), bf(448, W), bf(448, W),
                pltpu.SemaphoreType.DMA((5,)), pltpu.SemaphoreType.DMA((5,)),
            ],
        )(*parts)
    )


def solution(mesh):
    return jax.shard_map(
        shards,
        mesh=mesh,
        in_specs=(
            P(("gz", "gy"), "gx"),
            P(("gz", "gx"), "gy"),
            P(("gz", "gy"), "gx"),
            P(("gx", "gz"), "gy"),
            P(("gx", "gz"), "gy"),
        ),
        out_specs=(P(("gz", "gy"), "gx"), P(("gx", "gz"), "gy"), P(("gx", "gz"), "gy"), P("gy")),
        check_vma=False,
    )
```

```python
import jax
import jax.numpy as jnp
from jax import lax
from jax.experimental import pallas as pl
from jax.experimental.pallas import tpu as pltpu
from jax.sharding import PartitionSpec as P

MESH = pl.DeviceIdType.MESH
BF = jnp.bfloat16
F32 = jnp.float32
W = 896
N_SEMS = 160


def gelu_parts(pre):
    coeff = 0.7978845608028654
    inner = coeff * (pre + 0.044715 * pre * pre * pre)
    tangent = jnp.tanh(inner)
    value = 0.5 * pre * (1.0 + tangent)
    slope = 0.5 * (1.0 + tangent) + 0.5 * pre * (1.0 - tangent * tangent) * coeff * (
        1.0 + 3.0 * 0.044715 * pre * pre
    )
    return (value, slope)


def dot(left, right, dims):
    return lax.dot_general(left, right, (dims, ((), ())), preferred_element_type=F32)


class Ring:
    def __init__(self, me, device):
        self.me = me
        self.p, self.m, self.o = (lax.rem(me + k, 4) for k in (1, 3, 2))
        self.plus, self.minus = device(self.p), device(self.m)


def kernel(
    acts_hbm, pre_hbm, grad_hbm, w_in, w_out,
    o_ig, o_iw, o_ow, o_bias,
    acts, pre, grad,
    G, A, AC, D, WO, WI,
    HP, H1, H2, HX, HS, HB, ZR, SL,
    QP, Q1, Q2, QX, QS, ZS, ZL, IS, IR,
    ACC, WS, WR, BS, BR,
    send_sem, recv_sem, local_sem,
):
    gx, gy, gz = (lax.axis_index(name) for name in ("gx", "gy", "gz"))
    y, zl = gy // 2, lax.rem(gy, 2)
    zh, core = gz // 2, lax.rem(gz, 2)
    x = gx
    other = 1 - zl

    def dev(x_=x, y_=y, zl_=zl, zh_=zh, c_=core):
        return (x_, y_ * 2 + zl_, zh_ * 2 + c_)

    up, down, opp = (lax.rem(zh + k, 4) for k in (1, 3, 2))
    near = jnp.where(zl == 0, down, up)
    far = jnp.where(zl == 0, up, down)
    order = (zh, near, far, opp)
    ring = (zh, up, down, opp)
    twin = dev(c_=1 - core)
    pair = dev(zl_=other)
    rx = Ring(x, lambda k: dev(x_=k))
    ry = Ring(y, lambda k: dev(y_=k))

    peers = [rx.plus, rx.minus, ry.plus, ry.minus, twin, pair]
    peers += [dev(zh_=k) for k in (up, down, opp)]
    peers += [dev(zl_=other, zh_=near), dev(zl_=other, zh_=opp)]
    barrier = pltpu.get_barrier_semaphore()
    for peer in peers:
        pl.semaphore_signal(barrier, inc=1, device_id=peer, device_id_type=MESH)

    count = [0]
    sends = []

    def sem():
        count[0] += 1
        return count[0] - 1

    def send(k, src, dst, to):
        copy = pltpu.make_async_remote_copy(
            src_ref=src, dst_ref=dst, send_sem=send_sem.at[k], recv_sem=recv_sem.at[k],
            device_id=to, device_id_type=MESH,
        )
        copy.start()
        sends.append(copy)

    def arrived(k, dst):
        pltpu.make_async_remote_copy(
            src_ref=dst, dst_ref=dst, send_sem=send_sem.at[k], recv_sem=recv_sem.at[k],
            device_id=twin, device_id_type=MESH,
        ).wait_recv()

    n_local = [0]

    def local(src, dst):
        copy = pltpu.make_async_copy(src, dst, local_sem.at[n_local[0]])
        n_local[0] += 1
        copy.start()
        return copy

    staged = [local(a, b) for a, b in ((grad_hbm, grad), (pre_hbm, pre), (acts_hbm, acts))]

    def half(k):
        return pl.ds(pl.multiple_of(k * 32, 32), 32)

    LO, HI = pl.ds(0, 32), pl.ds(32, 32)

    class Rows:
        def __init__(self, src, buf):
            self.src, self.buf = src, buf
            self.k = [sem() for _ in range(6)]

        def columns(self, k):
            return self.src.at[:, pl.ds(pl.multiple_of(k * W, W), W)]

        def scatter(self):
            k, here = self.k, self.buf.at[zh, y, half(zl)]
            send(k[1], self.columns(far), here, dev(zh_=far))
            send(k[2], self.columns(near), here, dev(zl_=other, zh_=near))

        def scatter_rest(self):
            k, here = self.k, self.buf.at[zh, y, half(zl)]
            send(k[3], self.columns(opp), here, dev(zl_=other, zh_=opp))
            send(k[5], self.columns(opp), here, dev(zh_=opp))
            send(k[0], self.columns(zh), here, pair)
            self.own = local(self.columns(zh), here)

        def own_ready(self):
            self.own.wait()
            arrived(self.k[0], self.buf.at[zh, y, half(other)])

        def near_ready(self):
            block = self.buf.at[near, y]
            arrived(self.k[1], self.buf.at[near, y, half(zl)])
            arrived(self.k[2], self.buf.at[near, y, half(other)])
            send(self.k[4], block, block, pair)

        def far_ready(self):
            arrived(self.k[4], self.buf.at[far, y])

        def opp_ready(self):
            arrived(self.k[3], self.buf.at[opp, y, half(other)])
            arrived(self.k[5], self.buf.at[opp, y, half(zl)])

    class Gather:
        def __init__(self, buf, ring, s):
            self.buf, self.ring, self.s = buf, ring, s
            self.k = [sem() for _ in range(4)]

        def at(self, block, rows=pl.ds(0, 64)):
            return self.buf.at[self.s, block, rows]

        def start(self):
            r, mine = self.ring, self.at(self.ring.me)
            send(self.k[0], mine, mine, r.plus)
            send(self.k[1], mine, mine, r.minus)

        def forward(self):
            r = self.ring
            arrived(self.k[0], self.at(r.m))
            send(self.k[2], self.at(r.m, LO), self.at(r.m, LO), r.plus)
            arrived(self.k[1], self.at(r.p))
            send(self.k[3], self.at(r.p, HI), self.at(r.p, HI), r.minus)

        def done(self):
            r = self.ring
            arrived(self.k[2], self.at(r.o, LO))
            arrived(self.k[3], self.at(r.o, HI))

    class Scatter:
        def __init__(self, part, first, second, mixed, ring, t):
            self.part, self.first, self.second, self.mixed = (
                part.at[t], first.at[t], second.at[t], mixed.at[t]
            )
            self.ring = ring
            self.k = [sem() for _ in range(6)]

        def start(self):
            r, k = self.ring, self.k
            send(k[0], self.part.at[r.o, LO], self.first.at[0], r.plus)
            send(k[1], self.part.at[r.o, HI], self.first.at[1], r.minus)
            send(k[2], self.part.at[r.p, HI], self.second.at[0, HI], r.plus)
            send(k[3], self.part.at[r.m, LO], self.second.at[1, LO], r.minus)

        def middle(self):
            r, k = self.ring, self.k
            for way, rows, block, to in ((0, LO, r.p, r.plus), (1, HI, r.m, r.minus)):
                arrived(k[way], self.first.at[way])
                total = self.part[block, rows].astype(F32) + self.first[way].astype(F32)
                self.mixed[way] = total.astype(BF)
                send(k[4 + way], self.mixed.at[way], self.second.at[way, rows], to)

        def end(self):
            k = self.k
            arrived(k[2], self.second.at[0, HI])
            arrived(k[3], self.second.at[1, LO])
            arrived(k[4], self.second.at[0, LO])
            arrived(k[5], self.second.at[1, HI])
            return (
                self.part[self.ring.me].astype(F32)
                + self.second[0].astype(F32)
                + self.second[1].astype(F32)
            )

    class Depth:
        def __init__(self, buf):
            self.buf = buf
            self.k = [sem() for _ in range(4)]

        def start(self):
            mine = self.buf.at[zh, x]
            send(self.k[0], mine, mine, dev(zh_=up))
            send(self.k[1], mine, mine, dev(zh_=down))

        def forward(self):
            for k, came, rows, to in ((0, down, LO, up), (1, up, HI, down)):
                arrived(self.k[k], self.buf.at[came, x])
                piece = self.buf.at[came, x, rows]
                send(self.k[k + 2], piece, piece, dev(zh_=to))

        def done(self):
            arrived(self.k[2], self.buf.at[opp, x, LO])
            arrived(self.k[3], self.buf.at[opp, x, HI])

    rows_g, rows_a = Rows(grad, G), Rows(acts, A)
    g_y = [Gather(G, ry, s) for s in order]
    a_y = [Gather(A, ry, s) for s in order]
    c_z, c_x = Depth(AC), [Gather(AC, rx, s) for s in order]
    h_x = [Scatter(HP, H1, H2, HX, rx, t) for t in range(4)]
    h_k = [sem() for _ in range(3)]
    d_z, d_x = Depth(D), [Gather(D, rx, s) for s in ring]
    q_y = [Scatter(QP, Q1, Q2, QX, ry, t) for t in range(4)]
    q_k = [sem() for _ in range(4)]
    i_k = [sem() for _ in range(3)]
    w_k = [sem() for _ in range(2)]
    g_k = [sem() for _ in range(2)]
    b_k = sem()
    OWN, NEAR, FAR, OPP = range(4)
    UP, DOWN = 1, 2

    mine = pl.ds(pl.multiple_of(core * 448, 448), 448)
    theirs = pl.ds(pl.multiple_of((1 - core) * 448, 448), 448)
    own_w = [None, None]

    def weights(i, src, buf):
        send(w_k[i], src, buf.at[mine], twin)
        own_w[i] = local(src, buf.at[mine])

    def activations():
        staged[1].wait()
        value, slope = gelu_parts(pre[...].astype(F32))
        AC[zh, x] = value.astype(BF)
        SL[...] = slope

    def entry():
        pl.semaphore_wait(barrier, len(peers))
        staged[0].wait()

    def hidden(t, first=False):
        g_y[t].done()
        if first:
            own_w[0].wait()
            arrived(w_k[0], WO.at[theirs])
        part = dot(G[order[t]].reshape(256, W), WO[...], ((1,), (0,)))
        HP[t] = part.astype(BF).reshape(4, 64, W)
        h_x[t].start()

    def hidden_end(t):
        total = h_x[t].end()
        if t == OWN:
            HS[...] = total
        else:
            HB[t - 1] = total.astype(BF)
            send(h_k[t - 1], HB.at[t - 1], ZR.at[t - 1], dev(zh_=order[t]))

    def dh_rows():
        total = HS[...]
        for t in range(3):
            arrived(h_k[t], ZR.at[t])
            total = total + ZR[t].astype(F32)
        D[zh, x] = (total * SL[...]).astype(BF)

    def weight_grad(i, t, first=False):
        rows, cols = ((A, D), (G, AC))[i]
        s = ring[t] if i == 0 else order[t]
        right = cols[s].reshape(256, W)
        for low, size in ((0, 512), (512, 384)):
            left = rows[s, :, :, low : low + size].reshape(256, size)
            term = dot(left, right, ((0,), (0,)))
            if first:
                ACC[i, low : low + size] = term
            else:
                ACC[i, low : low + size] += term

    def share(i):
        WS[i] = ACC[i, theirs].astype(BF)
        send(g_k[i], WS.at[i], WR.at[i], twin)

    def inputs(t, first=False):
        d_x[t].done()
        if first:
            own_w[1].wait()
            arrived(w_k[1], WI.at[theirs])
        part = dot(D[ring[t]].reshape(256, W), WI[...], ((1,), (1,)))
        QP[t] = part.astype(BF).reshape(4, 64, W)
        q_y[t].start()

    def inputs_end(t):
        QS[t] = q_y[t].end()
        ZS[t] = QS[t, half(other)].astype(BF)
        send(q_k[t], ZS.at[t], ZL.at[t], pair)

    def inputs_out(t):
        arrived(q_k[t], ZL.at[t])
        total = (QS[t, half(zl)] + ZL[t].astype(F32)).astype(BF)
        if t == OWN:
            IR[zh] = total
        else:
            IS[t] = total
            send(i_k[t - 1], IS.at[t], IR.at[zh], dev(zh_=ring[t]))

    def bias_sums():
        BS[...] = jnp.sum(D[...].astype(F32).reshape(128, 8, W), axis=0)
        send(b_k, BS, BR, twin)

    def finish_bias():
        arrived(b_k, BR)
        o_bias[...] = jnp.sum(BS[...] + BR[...], axis=0)

    def finish_weight(i, out):
        arrived(g_k[i], WR.at[i])
        out[...] = (ACC[i, mine] + WR[i].astype(F32)).astype(BF)

    def finish_inputs():
        for t in range(1, 4):
            arrived(i_k[(None, 1, 0, 2)[t]], IR.at[ring[t]])
        for k in range(4):
            o_ig[:, k * W : (k + 1) * W] = IR[k]

    def finish_sends():
        for copy in sends:
            copy.wait_send()

    activations()
    entry()
    rows_g.scatter()
    weights(0, w_out, WO)
    c_x[OWN].start()
    rows_g.near_ready()
    g_y[NEAR].start()
    rows_g.scatter_rest()
    g_y[NEAR].forward()
    rows_g.far_ready()
    g_y[FAR].start()
    hidden(NEAR, True)
    rows_g.opp_ready()
    g_y[OPP].start()
    staged[2].wait()
    rows_a.scatter()
    rows_a.scatter_rest()
    g_y[FAR].forward()
    rows_g.own_ready()
    g_y[OWN].start()
    g_y[OPP].forward()
    hidden(FAR)
    h_x[NEAR].middle()
    g_y[OWN].forward()
    rows_a.near_ready()
    c_x[OWN].forward()
    c_z.start()
    hidden(OPP)
    h_x[FAR].middle()
    weights(1, w_in, WI)
    hidden(OWN)
    hidden_end(NEAR)
    rows_a.far_ready()
    a_y[NEAR].start()
    h_x[OPP].middle()
    c_z.forward()
    rows_a.opp_ready()
    a_y[FAR].start()
    hidden_end(FAR)
    h_x[OWN].middle()
    a_y[NEAR].forward()
    a_y[OPP].start()
    hidden_end(OPP)
    a_y[FAR].forward()
    rows_a.own_ready()
    a_y[OWN].start()
    c_x[NEAR].start()
    hidden_end(OWN)
    c_x[OWN].done()
    weight_grad(1, OWN, True)
    a_y[OPP].forward()
    dh_rows()
    d_x[OWN].start()
    d_z.start()
    a_y[OWN].forward()
    d_x[OWN].forward()
    c_x[NEAR].forward()
    d_z.forward()
    d_x[UP].start()
    inputs(OWN, True)
    for t in range(4):
        a_y[t].done()
    weight_grad(0, OWN, True)
    d_x[DOWN].start()
    d_x[UP].forward()
    d_z.done()
    d_x[OPP].start()
    q_y[OWN].middle()
    d_x[DOWN].forward()
    inputs(UP)
    inputs_end(OWN)
    d_x[OPP].forward()
    inputs(DOWN)
    q_y[UP].middle()
    c_x[FAR].start()
    inputs_out(OWN)
    inputs(OPP)
    q_y[DOWN].middle()
    inputs_end(UP)
    c_x[FAR].forward()
    c_z.done()
    c_x[OPP].start()
    weight_grad(0, UP)
    q_y[OPP].middle()
    inputs_end(DOWN)
    weight_grad(0, DOWN)
    inputs_out(UP)
    weight_grad(0, OPP)
    share(0)
    c_x[OPP].forward()
    inputs_end(OPP)
    inputs_out(DOWN)
    c_x[NEAR].done()
    weight_grad(1, NEAR)
    c_x[FAR].done()
    weight_grad(1, FAR)
    inputs_out(OPP)
    c_x[OPP].done()
    weight_grad(1, OPP)
    share(1)
    bias_sums()
    finish_weight(0, o_iw)
    finish_bias()
    finish_weight(1, o_ow)
    finish_inputs()
    finish_sends()


def shards(acts, preact, out_grad, w_in, w_out):
    vmem = pl.BlockSpec(memory_space=pltpu.VMEM)
    bf = lambda *shape: pltpu.VMEM(shape, BF)
    f32 = lambda *shape: pltpu.VMEM(shape, F32)
    scratch = dict(
        acts=bf(32, 4 * W), pre=bf(64, W), grad=bf(32, 4 * W),
        G=bf(4, 4, 64, W), A=bf(4, 4, 64, W), AC=bf(4, 4, 64, W), D=bf(4, 4, 64, W),
        WO=bf(W, W), WI=bf(W, W),
        HP=bf(4, 4, 64, W), H1=bf(4, 2, 32, W), H2=bf(4, 2, 64, W), HX=bf(4, 2, 32, W),
        HS=f32(64, W), HB=bf(3, 64, W), ZR=bf(3, 64, W), SL=f32(64, W),
        QP=bf(4, 4, 64, W), Q1=bf(4, 2, 32, W), Q2=bf(4, 2, 64, W), QX=bf(4, 2, 32, W),
        QS=f32(4, 64, W), ZS=bf(4, 32, W), ZL=bf(4, 32, W), IS=bf(4, 32, W), IR=bf(4, 32, W),
        ACC=f32(2, W, W), WS=bf(2, 448, W), WR=bf(2, 448, W),
        BS=f32(8, W), BR=f32(8, W),
        send_sem=pltpu.SemaphoreType.DMA((N_SEMS,)),
        recv_sem=pltpu.SemaphoreType.DMA((N_SEMS,)),
        local_sem=pltpu.SemaphoreType.DMA((16,)),
    )
    hbm = pl.BlockSpec(memory_space=pl.ANY)
    return pl.pallas_call(
        kernel,
        out_shape=(bf(32, 4 * W), bf(448, W), bf(448, W), f32(W)),
        in_specs=[hbm] * 5,
        out_specs=[vmem] * 4,
        scratch_shapes=list(scratch.values()),
        compiler_params=pltpu.CompilerParams(
            collective_id=0, has_side_effects=True, vmem_limit_bytes=60 * 2**20
        ),
    )(acts, preact, out_grad, w_in, w_out)


def solution(mesh):
    return jax.shard_map(
        shards,
        mesh=mesh,
        in_specs=(
            P(("gz", "gy"), "gx"),
            P(("gz", "gx"), "gy"),
            P(("gz", "gy"), "gx"),
            P(("gx", "gz"), "gy"),
            P(("gx", "gz"), "gy"),
        ),
        out_specs=(P(("gz", "gy"), "gx"), P(("gx", "gz"), "gy"), P(("gx", "gz"), "gy"), P("gy")),
        check_vma=False,
    )
```

```python
import jax
import jax.numpy as jnp
from jax import lax
from jax.experimental import pallas as pl
from jax.experimental.pallas import tpu as pltpu
from jax.sharding import PartitionSpec as P

MESH = pl.DeviceIdType.MESH
BF = jnp.bfloat16
F32 = jnp.float32
W = 896
N_SEMS = 150
N_SENDS = 40


def gelu_parts(pre):
    coeff = 0.7978845608028654
    inner = coeff * (pre + 0.044715 * pre * pre * pre)
    tangent = jnp.tanh(inner)
    value = 0.5 * pre * (1.0 + tangent)
    slope = 0.5 * (1.0 + tangent) + 0.5 * pre * (1.0 - tangent * tangent) * coeff * (
        1.0 + 3.0 * 0.044715 * pre * pre
    )
    return (value, slope)


def dot(left, right, dims):
    return lax.dot_general(left, right, (dims, ((), ())), preferred_element_type=F32)


class Ring:
    def __init__(self, me, device):
        self.me = me
        self.p, self.m, self.o = (lax.rem(me + k, 4) for k in (1, 3, 2))
        self.plus, self.minus = device(self.p), device(self.m)


def kernel(
    acts_hbm, pre_hbm, grad_hbm, w_in, w_out,
    o_ig, o_iw, o_ow, o_bias,
    acts, pre, grad,
    G, A, AC, D, WO, WI,
    HP, H1, H2, HX, HS, HB, ZR, SL,
    QP, Q1, Q2, QX, QS, ZS, ZL, IS, IR,
    ACC, WS, WR, BS, BR,
    send_sem, recv_sem, local_sem,
):
    gx, gy, gz = (lax.axis_index(name) for name in ("gx", "gy", "gz"))
    y, zl = gy // 2, lax.rem(gy, 2)
    zh, core = gz // 2, lax.rem(gz, 2)
    x = gx
    other = 1 - zl

    def dev(x_=x, y_=y, zl_=zl, zh_=zh, c_=core):
        return (x_, y_ * 2 + zl_, zh_ * 2 + c_)

    up, down, opp = (lax.rem(zh + k, 4) for k in (1, 3, 2))
    near = jnp.where(zl == 0, down, up)
    far = jnp.where(zl == 0, up, down)
    order = (zh, near, far, opp)
    ring = (zh, up, down, opp)
    twin = dev(c_=1 - core)
    pair = dev(zl_=other)
    rx = Ring(x, lambda k: dev(x_=k))
    ry = Ring(y, lambda k: dev(y_=k))

    peers = [rx.plus, rx.minus, ry.plus, ry.minus, twin, pair]
    peers += [dev(zh_=k) for k in (up, down, opp)]
    peers += [dev(zl_=other, zh_=near), dev(zl_=other, zh_=opp)]
    barrier = pltpu.get_barrier_semaphore()
    for peer in peers:
        pl.semaphore_signal(barrier, inc=1, device_id=peer, device_id_type=MESH)

    count = [0]
    sends = []

    def sem():
        count[0] += 1
        return count[0] - 1

    def send(k, src, dst, to):
        n = len(sends)
        if n >= N_SENDS:
            sends[n - N_SENDS].wait_send()
        copy = pltpu.make_async_remote_copy(
            src_ref=src, dst_ref=dst, send_sem=send_sem.at[n % N_SENDS], recv_sem=recv_sem.at[k],
            device_id=to, device_id_type=MESH,
        )
        copy.start()
        sends.append(copy)

    def arrived(k, dst):
        pltpu.make_async_remote_copy(
            src_ref=dst, dst_ref=dst, send_sem=send_sem.at[0], recv_sem=recv_sem.at[k],
            device_id=twin, device_id_type=MESH,
        ).wait_recv()

    n_local = [0]

    def local(src, dst):
        copy = pltpu.make_async_copy(src, dst, local_sem.at[n_local[0]])
        n_local[0] += 1
        copy.start()
        return copy

    staged = [local(a, b) for a, b in ((grad_hbm, grad), (pre_hbm, pre), (acts_hbm, acts))]

    def half(k):
        return pl.ds(pl.multiple_of(k * 32, 32), 32)

    LO, HI = pl.ds(0, 32), pl.ds(32, 32)

    class Rows:
        def __init__(self, src, buf):
            self.src, self.buf = src, buf
            self.k = [sem() for _ in range(6)]

        def columns(self, k):
            return self.src.at[:, pl.ds(pl.multiple_of(k * W, W), W)]

        def scatter(self):
            k, here = self.k, self.buf.at[zh, y, half(zl)]
            send(k[1], self.columns(far), here, dev(zh_=far))
            send(k[2], self.columns(near), here, dev(zl_=other, zh_=near))
            send(k[0], self.columns(zh), here, pair)
            self.own = local(self.columns(zh), here)

        def scatter_rest(self):
            k, here = self.k, self.buf.at[zh, y, half(zl)]
            send(k[3], self.columns(opp), here, dev(zl_=other, zh_=opp))
            send(k[5], self.columns(opp), here, dev(zh_=opp))

        def own_ready(self):
            self.own.wait()
            arrived(self.k[0], self.buf.at[zh, y, half(other)])

        def near_ready(self):
            block = self.buf.at[near, y]
            arrived(self.k[1], self.buf.at[near, y, half(zl)])
            arrived(self.k[2], self.buf.at[near, y, half(other)])
            send(self.k[4], block, block, pair)

        def far_ready(self):
            arrived(self.k[4], self.buf.at[far, y])

        def opp_ready(self):
            arrived(self.k[3], self.buf.at[opp, y, half(other)])
            arrived(self.k[5], self.buf.at[opp, y, half(zl)])

    class Gather:
        def __init__(self, buf, ring, s):
            self.buf, self.ring, self.s = buf, ring, s
            self.k = [sem() for _ in range(4)]

        def at(self, block, rows=pl.ds(0, 64)):
            return self.buf.at[self.s, block, rows]

        def start(self):
            r, mine = self.ring, self.at(self.ring.me)
            send(self.k[0], mine, mine, r.plus)
            send(self.k[1], mine, mine, r.minus)

        def forward(self):
            r = self.ring
            arrived(self.k[0], self.at(r.m))
            send(self.k[2], self.at(r.m, LO), self.at(r.m, LO), r.plus)
            arrived(self.k[1], self.at(r.p))
            send(self.k[3], self.at(r.p, HI), self.at(r.p, HI), r.minus)

        def done(self):
            r = self.ring
            arrived(self.k[2], self.at(r.o, LO))
            arrived(self.k[3], self.at(r.o, HI))

    class Scatter:
        def __init__(self, part, first, second, mixed, ring, t):
            self.part, self.first, self.second, self.mixed = (
                part.at[t], first.at[t], second.at[t], mixed.at[t]
            )
            self.ring = ring
            self.k = [sem() for _ in range(6)]

        def start(self):
            r, k = self.ring, self.k
            send(k[0], self.part.at[r.o, LO], self.first.at[0], r.plus)
            send(k[1], self.part.at[r.o, HI], self.first.at[1], r.minus)
            send(k[2], self.part.at[r.p, HI], self.second.at[0, HI], r.plus)
            send(k[3], self.part.at[r.m, LO], self.second.at[1, LO], r.minus)

        def middle(self):
            r, k = self.ring, self.k
            for way, rows, block, to in ((0, LO, r.p, r.plus), (1, HI, r.m, r.minus)):
                arrived(k[way], self.first.at[way])
                total = self.part[block, rows].astype(F32) + self.first[way].astype(F32)
                self.mixed[way] = total.astype(BF)
                send(k[4 + way], self.mixed.at[way], self.second.at[way, rows], to)

        def end(self):
            k = self.k
            arrived(k[2], self.second.at[0, HI])
            arrived(k[3], self.second.at[1, LO])
            arrived(k[4], self.second.at[0, LO])
            arrived(k[5], self.second.at[1, HI])
            return (
                self.part[self.ring.me].astype(F32)
                + self.second[0].astype(F32)
                + self.second[1].astype(F32)
            )

    class Depth:
        def __init__(self, buf):
            self.buf = buf
            self.k = [sem() for _ in range(4)]

        def start(self):
            mine = self.buf.at[zh, x]
            send(self.k[0], mine, mine, dev(zh_=up))
            send(self.k[1], mine, mine, dev(zh_=down))

        def forward(self):
            for k, came, rows, to in ((0, down, LO, up), (1, up, HI, down)):
                arrived(self.k[k], self.buf.at[came, x])
                piece = self.buf.at[came, x, rows]
                send(self.k[k + 2], piece, piece, dev(zh_=to))

        def done(self):
            arrived(self.k[2], self.buf.at[opp, x, LO])
            arrived(self.k[3], self.buf.at[opp, x, HI])

    rows_g, rows_a = Rows(grad, G), Rows(acts, A)
    g_y = [Gather(G, ry, s) for s in order]
    a_y = [Gather(A, ry, s) for s in order]
    c_z, c_x = Depth(AC), [Gather(AC, rx, s) for s in order]
    h_x = [Scatter(HP, H1, H2, HX, rx, t) for t in range(4)]
    h_k = [sem() for _ in range(3)]
    d_z, d_x = Depth(D), [Gather(D, rx, s) for s in ring]
    q_y = [Scatter(QP, Q1, Q2, QX, ry, t) for t in range(4)]
    q_k = [sem() for _ in range(4)]
    i_k = [sem() for _ in range(3)]
    w_k = [sem() for _ in range(2)]
    g_k = [sem() for _ in range(2)]
    b_k = sem()
    OWN, NEAR, FAR, OPP = range(4)
    UP, DOWN = 1, 2

    mine = pl.ds(pl.multiple_of(core * 448, 448), 448)
    theirs = pl.ds(pl.multiple_of((1 - core) * 448, 448), 448)
    own_w = [None, None]

    def weights(i, src, buf):
        send(w_k[i], src, buf.at[mine], twin)
        own_w[i] = local(src, buf.at[mine])

    def activations():
        staged[1].wait()
        value, slope = gelu_parts(pre[...].astype(F32))
        AC[zh, x] = value.astype(BF)
        SL[...] = slope

    def entry():
        pl.semaphore_wait(barrier, len(peers))
        staged[0].wait()

    def hidden(t, first=False):
        g_y[t].done()
        if first:
            own_w[0].wait()
            arrived(w_k[0], WO.at[theirs])
        part = dot(G[order[t]].reshape(256, W), WO[...], ((1,), (0,)))
        HP[t] = part.astype(BF).reshape(4, 64, W)
        h_x[t].start()

    def hidden_end(t):
        total = h_x[t].end()
        if t == OWN:
            HS[...] = total
        else:
            HB[t - 1] = total.astype(BF)
            send(h_k[t - 1], HB.at[t - 1], ZR.at[t - 1], dev(zh_=order[t]))

    def dh_rows():
        total = HS[...]
        for t in range(3):
            arrived(h_k[t], ZR.at[t])
            total = total + ZR[t].astype(F32)
        D[zh, x] = (total * SL[...]).astype(BF)

    def weight_grad(i, t, first=False):
        rows, cols = ((A, D), (G, AC))[i]
        s = ring[t] if i == 0 else order[t]
        right = cols[s].reshape(256, W)
        for low, size in ((0, 512), (512, 384)):
            left = rows[s, :, :, low : low + size].reshape(256, size)
            term = dot(left, right, ((0,), (0,)))
            if first:
                ACC[i, low : low + size] = term
            else:
                ACC[i, low : low + size] += term

    def share(i):
        WS[i] = ACC[i, theirs].astype(BF)
        send(g_k[i], WS.at[i], WR.at[i], twin)

    def inputs(t, first=False):
        d_x[t].done()
        if first:
            own_w[1].wait()
            arrived(w_k[1], WI.at[theirs])
        part = dot(D[ring[t]].reshape(256, W), WI[...], ((1,), (1,)))
        QP[t] = part.astype(BF).reshape(4, 64, W)
        q_y[t].start()

    def inputs_end(t):
        QS[t] = q_y[t].end()
        ZS[t] = QS[t, half(other)].astype(BF)
        send(q_k[t], ZS.at[t], ZL.at[t], pair)

    def inputs_out(t):
        arrived(q_k[t], ZL.at[t])
        total = (QS[t, half(zl)] + ZL[t].astype(F32)).astype(BF)
        if t == OWN:
            IR[zh] = total
        else:
            IS[t] = total
            send(i_k[t - 1], IS.at[t], IR.at[zh], dev(zh_=ring[t]))

    def bias_sums():
        BS[...] = jnp.sum(D[...].astype(F32).reshape(128, 8, W), axis=0)
        send(b_k, BS, BR, twin)

    def finish_bias():
        arrived(b_k, BR)
        o_bias[...] = jnp.sum(BS[...] + BR[...], axis=0)

    def finish_weight(i, out):
        arrived(g_k[i], WR.at[i])
        out[...] = (ACC[i, mine] + WR[i].astype(F32)).astype(BF)

    def finish_inputs():
        for t in range(1, 4):
            arrived(i_k[(None, 1, 0, 2)[t]], IR.at[ring[t]])
        for k in range(4):
            o_ig[:, k * W : (k + 1) * W] = IR[k]

    def finish_sends():
        for copy in sends[-N_SENDS:]:
            copy.wait_send()

    activations()
    entry()
    rows_g.scatter()
    weights(0, w_out, WO)
    rows_g.near_ready()
    g_y[NEAR].start()
    rows_g.scatter_rest()
    c_x[OWN].start()
    rows_g.own_ready()
    g_y[NEAR].forward()
    rows_g.far_ready()
    g_y[FAR].start()
    hidden(NEAR, True)
    rows_g.opp_ready()
    g_y[OPP].start()
    c_z.start()
    g_y[FAR].forward()
    g_y[OWN].start()
    staged[2].wait()
    rows_a.scatter()
    rows_a.scatter_rest()
    h_x[NEAR].middle()
    g_y[OPP].forward()
    hidden(FAR)
    c_x[OWN].forward()
    g_y[OWN].forward()
    hidden(OPP)
    rows_a.near_ready()
    h_x[FAR].middle()
    hidden_end(NEAR)
    c_z.forward()
    hidden(OWN)
    h_x[OPP].middle()
    a_y[NEAR].start()
    hidden_end(FAR)
    h_x[OWN].middle()
    hidden_end(OPP)
    weights(1, w_in, WI)
    hidden_end(OWN)
    c_x[NEAR].start()
    rows_a.far_ready()
    a_y[FAR].start()
    rows_a.opp_ready()
    a_y[NEAR].forward()
    a_y[OPP].start()
    c_x[OWN].done()
    weight_grad(1, OWN, True)
    c_x[FAR].start()
    rows_a.own_ready()
    dh_rows()
    d_x[OWN].start()
    d_z.start()
    a_y[FAR].forward()
    a_y[OWN].start()
    d_x[OWN].forward()
    c_x[NEAR].forward()
    c_x[FAR].forward()
    a_y[OPP].forward()
    d_z.forward()
    d_x[UP].start()
    inputs(OWN, True)
    a_y[OWN].forward()
    d_x[DOWN].start()
    d_x[UP].forward()
    d_z.done()
    d_x[OPP].start()
    q_y[OWN].middle()
    d_x[DOWN].forward()
    inputs(UP)
    inputs_end(OWN)
    d_x[OPP].forward()
    c_z.done()
    c_x[OPP].start()
    inputs(DOWN)
    q_y[UP].middle()
    inputs_out(OWN)
    for t in range(4):
        a_y[t].done()
    weight_grad(0, OWN, True)
    weight_grad(0, UP)
    inputs(OPP)
    q_y[DOWN].middle()
    inputs_end(UP)
    weight_grad(0, DOWN)
    weight_grad(0, OPP)
    share(0)
    c_x[OPP].forward()
    q_y[OPP].middle()
    inputs_end(DOWN)
    bias_sums()
    c_x[NEAR].done()
    weight_grad(1, NEAR)
    inputs_end(OPP)
    inputs_out(UP)
    c_x[FAR].done()
    weight_grad(1, FAR)
    inputs_out(DOWN)
    c_x[OPP].done()
    weight_grad(1, OPP)
    share(1)
    inputs_out(OPP)
    finish_weight(0, o_iw)
    finish_bias()
    finish_weight(1, o_ow)
    finish_inputs()
    finish_sends()


def shards(acts, preact, out_grad, w_in, w_out):
    vmem = pl.BlockSpec(memory_space=pltpu.VMEM)
    bf = lambda *shape: pltpu.VMEM(shape, BF)
    f32 = lambda *shape: pltpu.VMEM(shape, F32)
    scratch = dict(
        acts=bf(32, 4 * W), pre=bf(64, W), grad=bf(32, 4 * W),
        G=bf(4, 4, 64, W), A=bf(4, 4, 64, W), AC=bf(4, 4, 64, W), D=bf(4, 4, 64, W),
        WO=bf(W, W), WI=bf(W, W),
        HP=bf(4, 4, 64, W), H1=bf(4, 2, 32, W), H2=bf(4, 2, 64, W), HX=bf(4, 2, 32, W),
        HS=f32(64, W), HB=bf(3, 64, W), ZR=bf(3, 64, W), SL=f32(64, W),
        QP=bf(4, 4, 64, W), Q1=bf(4, 2, 32, W), Q2=bf(4, 2, 64, W), QX=bf(4, 2, 32, W),
        QS=f32(4, 64, W), ZS=bf(4, 32, W), ZL=bf(4, 32, W), IS=bf(4, 32, W), IR=bf(4, 32, W),
        ACC=f32(2, W, W), WS=bf(2, 448, W), WR=bf(2, 448, W),
        BS=f32(8, W), BR=f32(8, W),
        send_sem=pltpu.SemaphoreType.DMA((N_SENDS,)),
        recv_sem=pltpu.SemaphoreType.DMA((N_SEMS,)),
        local_sem=pltpu.SemaphoreType.DMA((16,)),
    )
    hbm = pl.BlockSpec(memory_space=pl.ANY)
    return pl.pallas_call(
        kernel,
        out_shape=(bf(32, 4 * W), bf(448, W), bf(448, W), f32(W)),
        in_specs=[hbm] * 5,
        out_specs=[vmem] * 4,
        scratch_shapes=list(scratch.values()),
        compiler_params=pltpu.CompilerParams(
            collective_id=0, has_side_effects=True, vmem_limit_bytes=60 * 2**20
        ),
    )(acts, preact, out_grad, w_in, w_out)


def solution(mesh):
    return jax.shard_map(
        shards,
        mesh=mesh,
        in_specs=(
            P(("gz", "gy"), "gx"),
            P(("gz", "gx"), "gy"),
            P(("gz", "gy"), "gx"),
            P(("gx", "gz"), "gy"),
            P(("gx", "gz"), "gy"),
        ),
        out_specs=(P(("gz", "gy"), "gx"), P(("gx", "gz"), "gy"), P(("gx", "gz"), "gy"), P("gy")),
        check_vma=False,
    )
```

```python
import jax
import jax.numpy as jnp
from jax import lax
from jax.experimental import pallas as pl
from jax.experimental.pallas import tpu as pltpu
from jax.sharding import PartitionSpec as P

MESH = pl.DeviceIdType.MESH
BF = jnp.bfloat16
F32 = jnp.float32
W = 896
N_SEMS = 150
N_SENDS = 40


def gelu_parts(pre):
    coeff = 0.7978845608028654
    inner = coeff * (pre + 0.044715 * pre * pre * pre)
    tangent = jnp.tanh(inner)
    value = 0.5 * pre * (1.0 + tangent)
    slope = 0.5 * (1.0 + tangent) + 0.5 * pre * (1.0 - tangent * tangent) * coeff * (
        1.0 + 3.0 * 0.044715 * pre * pre
    )
    return (value, slope)


def dot(left, right, dims):
    return lax.dot_general(left, right, (dims, ((), ())), preferred_element_type=F32)


class Ring:
    def __init__(self, me, device):
        self.me = me
        self.p, self.m, self.o = (lax.rem(me + k, 4) for k in (1, 3, 2))
        self.plus, self.minus = device(self.p), device(self.m)


def kernel(
    acts_hbm, pre_hbm, grad_hbm, w_in, w_out,
    o_ig, o_iw, o_ow, o_bias,
    acts, pre, grad,
    G, A, AC, D, WO, WI,
    HP, H1, H2, HX, HS, HB, ZR, SL,
    QP, Q1, Q2, QX, QS, ZS, ZL, IS, IR,
    ACC, WS, WR, BS, BR,
    send_sem, recv_sem, local_sem,
):
    gx, gy, gz = (lax.axis_index(name) for name in ("gx", "gy", "gz"))
    y, zl = gy // 2, lax.rem(gy, 2)
    zh, core = gz // 2, lax.rem(gz, 2)
    x = gx
    other = 1 - zl

    def dev(x_=x, y_=y, zl_=zl, zh_=zh, c_=core):
        return (x_, y_ * 2 + zl_, zh_ * 2 + c_)

    up, down, opp = (lax.rem(zh + k, 4) for k in (1, 3, 2))
    near = jnp.where(zl == 0, down, up)
    far = jnp.where(zl == 0, up, down)
    order = (zh, near, far, opp)
    ring = (zh, up, down, opp)
    twin = dev(c_=1 - core)
    pair = dev(zl_=other)
    rx = Ring(x, lambda k: dev(x_=k))
    ry = Ring(y, lambda k: dev(y_=k))

    peers = [rx.plus, rx.minus, ry.plus, ry.minus, twin, pair]
    peers += [dev(zh_=k) for k in (up, down, opp)]
    peers += [dev(zl_=other, zh_=near), dev(zl_=other, zh_=opp)]
    barrier = pltpu.get_barrier_semaphore()
    for peer in peers:
        pl.semaphore_signal(barrier, inc=1, device_id=peer, device_id_type=MESH)

    count = [0]
    sends = []

    def sem():
        count[0] += 1
        return count[0] - 1

    def send(k, src, dst, to):
        n = len(sends)
        if n >= N_SENDS:
            sends[n - N_SENDS].wait_send()
        copy = pltpu.make_async_remote_copy(
            src_ref=src, dst_ref=dst, send_sem=send_sem.at[n % N_SENDS], recv_sem=recv_sem.at[k],
            device_id=to, device_id_type=MESH,
        )
        copy.start()
        sends.append(copy)

    def arrived(k, dst):
        pltpu.make_async_remote_copy(
            src_ref=dst, dst_ref=dst, send_sem=send_sem.at[0], recv_sem=recv_sem.at[k],
            device_id=twin, device_id_type=MESH,
        ).wait_recv()

    n_local = [0]

    def local(src, dst):
        copy = pltpu.make_async_copy(src, dst, local_sem.at[n_local[0]])
        n_local[0] += 1
        copy.start()
        return copy

    staged = [local(a, b) for a, b in ((grad_hbm, grad), (pre_hbm, pre), (acts_hbm, acts))]

    def half(k):
        return pl.ds(pl.multiple_of(k * 32, 32), 32)

    LO, HI = pl.ds(0, 32), pl.ds(32, 32)

    class Rows:
        def __init__(self, src, buf):
            self.src, self.buf = src, buf
            self.k = [sem() for _ in range(6)]

        def columns(self, k):
            return self.src.at[:, pl.ds(pl.multiple_of(k * W, W), W)]

        def scatter(self):
            k, here = self.k, self.buf.at[zh, y, half(zl)]
            send(k[1], self.columns(far), here, dev(zh_=far))
            send(k[2], self.columns(near), here, dev(zl_=other, zh_=near))
            send(k[0], self.columns(zh), here, pair)
            self.own = local(self.columns(zh), here)

        def scatter_rest(self):
            k, here = self.k, self.buf.at[zh, y, half(zl)]
            send(k[3], self.columns(opp), here, dev(zl_=other, zh_=opp))
            send(k[5], self.columns(opp), here, dev(zh_=opp))

        def own_ready(self):
            self.own.wait()
            arrived(self.k[0], self.buf.at[zh, y, half(other)])

        def near_ready(self):
            block = self.buf.at[near, y]
            arrived(self.k[1], self.buf.at[near, y, half(zl)])
            arrived(self.k[2], self.buf.at[near, y, half(other)])
            send(self.k[4], block, block, pair)

        def far_ready(self):
            arrived(self.k[4], self.buf.at[far, y])

        def opp_ready(self):
            arrived(self.k[3], self.buf.at[opp, y, half(other)])
            arrived(self.k[5], self.buf.at[opp, y, half(zl)])

    class Gather:
        def __init__(self, buf, ring, s):
            self.buf, self.ring, self.s = buf, ring, s
            self.k = [sem() for _ in range(4)]

        def at(self, block, rows=pl.ds(0, 64)):
            return self.buf.at[self.s, block, rows]

        def start(self):
            r, mine = self.ring, self.at(self.ring.me)
            send(self.k[0], mine, mine, r.plus)
            send(self.k[1], mine, mine, r.minus)

        def forward(self):
            r = self.ring
            arrived(self.k[0], self.at(r.m))
            send(self.k[2], self.at(r.m, LO), self.at(r.m, LO), r.plus)
            arrived(self.k[1], self.at(r.p))
            send(self.k[3], self.at(r.p, HI), self.at(r.p, HI), r.minus)

        def done(self):
            r = self.ring
            arrived(self.k[2], self.at(r.o, LO))
            arrived(self.k[3], self.at(r.o, HI))

    class Scatter:
        def __init__(self, part, first, second, mixed, ring, t):
            self.part, self.first, self.second, self.mixed = (
                part.at[t], first.at[t], second.at[t], mixed.at[t]
            )
            self.ring = ring
            self.k = [sem() for _ in range(6)]

        def start(self):
            r, k = self.ring, self.k
            send(k[0], self.part.at[r.o, LO], self.first.at[0], r.plus)
            send(k[1], self.part.at[r.o, HI], self.first.at[1], r.minus)
            send(k[2], self.part.at[r.p, HI], self.second.at[0, HI], r.plus)
            send(k[3], self.part.at[r.m, LO], self.second.at[1, LO], r.minus)

        def middle(self):
            r, k = self.ring, self.k
            for way, rows, block, to in ((0, LO, r.p, r.plus), (1, HI, r.m, r.minus)):
                arrived(k[way], self.first.at[way])
                total = self.part[block, rows].astype(F32) + self.first[way].astype(F32)
                self.mixed[way] = total.astype(BF)
                send(k[4 + way], self.mixed.at[way], self.second.at[way, rows], to)

        def end(self):
            k = self.k
            arrived(k[2], self.second.at[0, HI])
            arrived(k[3], self.second.at[1, LO])
            arrived(k[4], self.second.at[0, LO])
            arrived(k[5], self.second.at[1, HI])
            return (
                self.part[self.ring.me].astype(F32)
                + self.second[0].astype(F32)
                + self.second[1].astype(F32)
            )

    class Depth:
        def __init__(self, buf):
            self.buf = buf
            self.k = [sem() for _ in range(4)]

        def start(self):
            mine = self.buf.at[zh, x]
            send(self.k[0], mine, mine, dev(zh_=up))
            send(self.k[1], mine, mine, dev(zh_=down))

        def forward(self):
            for k, came, rows, to in ((0, down, LO, up), (1, up, HI, down)):
                arrived(self.k[k], self.buf.at[came, x])
                piece = self.buf.at[came, x, rows]
                send(self.k[k + 2], piece, piece, dev(zh_=to))

        def done(self):
            arrived(self.k[2], self.buf.at[opp, x, LO])
            arrived(self.k[3], self.buf.at[opp, x, HI])

    rows_g, rows_a = Rows(grad, G), Rows(acts, A)
    g_y = [Gather(G, ry, s) for s in order]
    a_y = [Gather(A, ry, s) for s in order]
    c_z, c_x = Depth(AC), [Gather(AC, rx, s) for s in order]
    h_x = [Scatter(HP, H1, H2, HX, rx, t) for t in range(4)]
    h_k = [sem() for _ in range(3)]
    d_z, d_x = Depth(D), [Gather(D, rx, s) for s in ring]
    q_y = [Scatter(QP, Q1, Q2, QX, ry, t) for t in range(4)]
    q_k = [sem() for _ in range(4)]
    i_k = [sem() for _ in range(3)]
    w_k = [sem() for _ in range(2)]
    g_k = [sem() for _ in range(2)]
    b_k = sem()
    OWN, NEAR, FAR, OPP = range(4)
    UP, DOWN = 1, 2

    mine = pl.ds(pl.multiple_of(core * 448, 448), 448)
    theirs = pl.ds(pl.multiple_of((1 - core) * 448, 448), 448)
    own_w = [None, None]

    def weights(i, src, buf):
        send(w_k[i], src, buf.at[mine], twin)
        own_w[i] = local(src, buf.at[mine])

    def activations():
        staged[1].wait()
        value, slope = gelu_parts(pre[...].astype(F32))
        AC[zh, x] = value.astype(BF)
        SL[...] = slope

    def entry():
        pl.semaphore_wait(barrier, len(peers))
        staged[0].wait()

    def hidden(t, first=False):
        g_y[t].done()
        if first:
            own_w[0].wait()
            arrived(w_k[0], WO.at[theirs])
        part = dot(G[order[t]].reshape(256, W), WO[...], ((1,), (0,)))
        HP[t] = part.astype(BF).reshape(4, 64, W)
        h_x[t].start()

    def hidden_end(t):
        total = h_x[t].end()
        if t == OWN:
            HS[...] = total
        else:
            HB[t - 1] = total.astype(BF)
            send(h_k[t - 1], HB.at[t - 1], ZR.at[t - 1], dev(zh_=order[t]))

    def dh_rows():
        total = HS[...]
        for t in range(3):
            arrived(h_k[t], ZR.at[t])
            total = total + ZR[t].astype(F32)
        D[zh, x] = (total * SL[...]).astype(BF)

    def weight_grad(i, t, first=False):
        rows, cols = ((A, D), (G, AC))[i]
        s = ring[t] if i == 0 else order[t]
        right = cols[s].reshape(256, W)
        for low, size in ((0, 512), (512, 384)):
            left = rows[s, :, :, low : low + size].reshape(256, size)
            term = dot(left, right, ((0,), (0,)))
            if first:
                ACC[i, low : low + size] = term
            else:
                ACC[i, low : low + size] += term

    def share(i):
        WS[i] = ACC[i, theirs].astype(BF)
        send(g_k[i], WS.at[i], WR.at[i], twin)

    def inputs(t, first=False):
        d_x[t].done()
        if first:
            own_w[1].wait()
            arrived(w_k[1], WI.at[theirs])
        part = dot(D[ring[t]].reshape(256, W), WI[...], ((1,), (1,)))
        QP[t] = part.astype(BF).reshape(4, 64, W)
        q_y[t].start()

    def inputs_end(t):
        QS[t] = q_y[t].end()
        ZS[t] = QS[t, half(other)].astype(BF)
        send(q_k[t], ZS.at[t], ZL.at[t], pair)

    def inputs_out(t):
        arrived(q_k[t], ZL.at[t])
        total = (QS[t, half(zl)] + ZL[t].astype(F32)).astype(BF)
        if t == OWN:
            IR[zh] = total
        else:
            IS[t] = total
            send(i_k[t - 1], IS.at[t], IR.at[zh], dev(zh_=ring[t]))

    def bias_sums():
        BS[...] = jnp.sum(D[...].astype(F32).reshape(128, 8, W), axis=0)
        send(b_k, BS, BR, twin)

    def finish_bias():
        arrived(b_k, BR)
        o_bias[...] = jnp.sum(BS[...] + BR[...], axis=0)

    def finish_weight(i, out):
        arrived(g_k[i], WR.at[i])
        out[...] = (ACC[i, mine] + WR[i].astype(F32)).astype(BF)

    def finish_inputs():
        for t in range(1, 4):
            arrived(i_k[(None, 1, 0, 2)[t]], IR.at[ring[t]])
        for k in range(4):
            o_ig[:, k * W : (k + 1) * W] = IR[k]

    def finish_sends():
        for copy in sends[-N_SENDS:]:
            copy.wait_send()

    activations()
    entry()
    rows_g.scatter()
    weights(0, w_out, WO)
    rows_g.near_ready()
    g_y[NEAR].start()
    rows_g.scatter_rest()
    c_x[OWN].start()
    rows_g.own_ready()
    g_y[NEAR].forward()
    rows_g.far_ready()
    g_y[FAR].start()
    hidden(NEAR, True)
    rows_g.opp_ready()
    g_y[OPP].start()
    c_z.start()
    g_y[FAR].forward()
    staged[2].wait()
    rows_a.scatter()
    rows_a.scatter_rest()
    h_x[NEAR].middle()
    g_y[OWN].start()
    g_y[OPP].forward()
    hidden(FAR)
    c_x[OWN].forward()
    g_y[OWN].forward()
    hidden(OPP)
    rows_a.near_ready()
    h_x[FAR].middle()
    hidden_end(NEAR)
    c_z.forward()
    hidden(OWN)
    h_x[OPP].middle()
    a_y[NEAR].start()
    hidden_end(FAR)
    h_x[OWN].middle()
    hidden_end(OPP)
    weights(1, w_in, WI)
    hidden_end(OWN)
    c_x[NEAR].start()
    rows_a.far_ready()
    a_y[FAR].start()
    rows_a.opp_ready()
    a_y[NEAR].forward()
    a_y[OPP].start()
    c_x[OWN].done()
    weight_grad(1, OWN, True)
    c_x[FAR].start()
    rows_a.own_ready()
    dh_rows()
    d_x[OWN].start()
    d_z.start()
    a_y[FAR].forward()
    a_y[OWN].start()
    d_x[OWN].forward()
    a_y[OPP].forward()
    d_z.forward()
    d_x[UP].start()
    inputs(OWN, True)
    a_y[OWN].forward()
    d_x[DOWN].start()
    d_x[UP].forward()
    d_z.done()
    d_x[OPP].start()
    q_y[OWN].middle()
    d_x[DOWN].forward()
    inputs(UP)
    inputs_end(OWN)
    d_x[OPP].forward()
    c_x[NEAR].forward()
    c_x[FAR].forward()
    c_z.done()
    c_x[OPP].start()
    inputs(DOWN)
    q_y[UP].middle()
    inputs_out(OWN)
    for t in range(4):
        a_y[t].done()
    weight_grad(0, OWN, True)
    weight_grad(0, UP)
    inputs(OPP)
    q_y[DOWN].middle()
    inputs_end(UP)
    weight_grad(0, DOWN)
    weight_grad(0, OPP)
    share(0)
    c_x[OPP].forward()
    q_y[OPP].middle()
    inputs_end(DOWN)
    bias_sums()
    c_x[NEAR].done()
    weight_grad(1, NEAR)
    inputs_end(OPP)
    inputs_out(UP)
    c_x[FAR].done()
    weight_grad(1, FAR)
    inputs_out(DOWN)
    c_x[OPP].done()
    weight_grad(1, OPP)
    share(1)
    inputs_out(OPP)
    finish_weight(0, o_iw)
    finish_bias()
    finish_weight(1, o_ow)
    finish_inputs()
    finish_sends()


def deliver(from_ig, from_iw, from_ow, from_bias, o_ig, o_iw, o_ow, o_bias, sem):
    pieces = [(from_bias, o_bias)]
    for src, dst, rows in ((from_iw, o_iw, 224), (from_ow, o_ow, 224), (from_ig, o_ig, 16)):
        for k in range(src.shape[0] // rows):
            at = pl.ds(k * rows, rows)
            pieces.append((src.at[at], dst.at[at]))
    copies = [pltpu.make_async_copy(a, b, sem.at[k]) for k, (a, b) in enumerate(pieces)]
    for copy in copies:
        copy.start()
    for copy in copies:
        copy.wait()


def shards(acts, preact, out_grad, w_in, w_out):
    vmem = pl.BlockSpec(memory_space=pltpu.VMEM)
    bf = lambda *shape: pltpu.VMEM(shape, BF)
    f32 = lambda *shape: pltpu.VMEM(shape, F32)
    scratch = dict(
        acts=bf(32, 4 * W), pre=bf(64, W), grad=bf(32, 4 * W),
        G=bf(4, 4, 64, W), A=bf(4, 4, 64, W), AC=bf(4, 4, 64, W), D=bf(4, 4, 64, W),
        WO=bf(W, W), WI=bf(W, W),
        HP=bf(4, 4, 64, W), H1=bf(4, 2, 32, W), H2=bf(4, 2, 64, W), HX=bf(4, 2, 32, W),
        HS=f32(64, W), HB=bf(3, 64, W), ZR=bf(3, 64, W), SL=f32(64, W),
        QP=bf(4, 4, 64, W), Q1=bf(4, 2, 32, W), Q2=bf(4, 2, 64, W), QX=bf(4, 2, 32, W),
        QS=f32(4, 64, W), ZS=bf(4, 32, W), ZL=bf(4, 32, W), IS=bf(4, 32, W), IR=bf(4, 32, W),
        ACC=f32(2, W, W), WS=bf(2, 448, W), WR=bf(2, 448, W),
        BS=f32(8, W), BR=f32(8, W),
        send_sem=pltpu.SemaphoreType.DMA((N_SENDS,)),
        recv_sem=pltpu.SemaphoreType.DMA((N_SEMS,)),
        local_sem=pltpu.SemaphoreType.DMA((16,)),
    )
    hbm = pl.BlockSpec(memory_space=pl.ANY)
    parts = pl.pallas_call(
        kernel,
        out_shape=(bf(32, 4 * W), bf(448, W), bf(448, W), f32(W)),
        in_specs=[hbm] * 5,
        out_specs=[vmem] * 4,
        scratch_shapes=list(scratch.values()),
        compiler_params=pltpu.CompilerParams(
            collective_id=0, has_side_effects=True, vmem_limit_bytes=60 * 2**20
        ),
    )(acts, preact, out_grad, w_in, w_out)
    return pl.pallas_call(
        deliver,
        out_shape=tuple(jax.ShapeDtypeStruct(p.shape, p.dtype) for p in parts),
        in_specs=[vmem] * 4,
        out_specs=[hbm] * 4,
        scratch_shapes=[pltpu.SemaphoreType.DMA((7,))],
        compiler_params=pltpu.CompilerParams(vmem_limit_bytes=2**20),
    )(*parts)


def solution(mesh):
    return jax.shard_map(
        shards,
        mesh=mesh,
        in_specs=(
            P(("gz", "gy"), "gx"),
            P(("gz", "gx"), "gy"),
            P(("gz", "gy"), "gx"),
            P(("gx", "gz"), "gy"),
            P(("gx", "gz"), "gy"),
        ),
        out_specs=(P(("gz", "gy"), "gx"), P(("gx", "gz"), "gy"), P(("gx", "gz"), "gy"), P("gy")),
        check_vma=False,
    )
```

```python
import jax
import jax.numpy as jnp
from jax import lax
from jax.experimental import pallas as pl
from jax.experimental.pallas import tpu as pltpu
from jax.sharding import PartitionSpec as P

MESH = pl.DeviceIdType.MESH
BF = jnp.bfloat16
F32 = jnp.float32
W = 896
N_SEMS = 100
N_SENDS = 32


def gelu_parts(pre):
    coeff = 0.7978845608028654
    inner = coeff * (pre + 0.044715 * pre * pre * pre)
    tangent = jnp.tanh(inner)
    value = 0.5 * pre * (1.0 + tangent)
    slope = 0.5 * (1.0 + tangent) + 0.5 * pre * (1.0 - tangent * tangent) * coeff * (
        1.0 + 3.0 * 0.044715 * pre * pre
    )
    return (value, slope)


def dot(left, right, dims):
    return lax.dot_general(left, right, (dims, ((), ())), preferred_element_type=F32)


class Ring:
    def __init__(self, me, device):
        self.me = me
        self.p, self.m, self.o = (lax.rem(me + k, 4) for k in (1, 3, 2))
        self.plus, self.minus = device(self.p), device(self.m)


def kernel(
    acts_hbm, pre_hbm, grad_hbm, w_in, w_out,
    o_ig, o_iw, o_ow, o_bias,
    acts, pre, grad,
    G, A, AC, D, WO, WI,
    HP, H1, H2, HX, HS, HB, ZR, SL,
    QP, Q1, Q2, QX, QS, ZS, ZL, IS, IR,
    ACC, WS, WR, BS, BR,
    send_sem, recv_sem, local_sem,
):
    gx, gy, gz = (lax.axis_index(name) for name in ("gx", "gy", "gz"))
    y, zl = gy // 2, lax.rem(gy, 2)
    zh, core = gz // 2, lax.rem(gz, 2)
    x = gx
    other = 1 - zl

    def dev(x_=x, y_=y, zl_=zl, zh_=zh, c_=core):
        return (x_, y_ * 2 + zl_, zh_ * 2 + c_)

    up, down, opp = (lax.rem(zh + k, 4) for k in (1, 3, 2))
    near = jnp.where(zl == 0, down, up)
    far = jnp.where(zl == 0, up, down)
    order = (zh, near, far, opp)
    ring = (zh, up, down, opp)
    twin = dev(c_=1 - core)
    pair = dev(zl_=other)
    rx = Ring(x, lambda k: dev(x_=k))
    ry = Ring(y, lambda k: dev(y_=k))

    peers = [rx.plus, rx.minus, ry.plus, ry.minus, twin, pair]
    peers += [dev(zh_=k) for k in (up, down, opp)]
    peers += [dev(zl_=other, zh_=near), dev(zl_=other, zh_=opp)]
    barrier = pltpu.get_barrier_semaphore()
    for peer in peers:
        pl.semaphore_signal(barrier, inc=1, device_id=peer, device_id_type=MESH)

    count = [0]
    sends = []

    def sem():
        count[0] += 1
        return count[0] - 1

    def send(k, src, dst, to):
        n = len(sends)
        if n >= N_SENDS:
            sends[n - N_SENDS].wait_send()
        copy = pltpu.make_async_remote_copy(
            src_ref=src, dst_ref=dst, send_sem=send_sem.at[n % N_SENDS], recv_sem=recv_sem.at[k],
            device_id=to, device_id_type=MESH,
        )
        copy.start()
        sends.append(copy)

    def arrived(k, dst):
        pltpu.make_async_remote_copy(
            src_ref=dst, dst_ref=dst, send_sem=send_sem.at[0], recv_sem=recv_sem.at[k],
            device_id=twin, device_id_type=MESH,
        ).wait_recv()

    n_local = [0]

    def local(src, dst):
        copy = pltpu.make_async_copy(src, dst, local_sem.at[n_local[0]])
        n_local[0] += 1
        copy.start()
        return copy

    staged = [local(a, b) for a, b in ((grad_hbm, grad), (pre_hbm, pre), (acts_hbm, acts))]

    def half(k):
        return pl.ds(pl.multiple_of(k * 32, 32), 32)

    LO, HI = pl.ds(0, 32), pl.ds(32, 32)

    class Rows:
        def __init__(self, src, buf):
            self.src, self.buf = src, buf
            self.k = [sem() for _ in range(4)]

        def columns(self, k):
            return self.src.at[:, pl.ds(pl.multiple_of(k * W, W), W)]

        def scatter(self):
            k, here = self.k, self.buf.at[zh, y, half(zl)]
            send(k[1], self.columns(far), here, dev(zh_=far))
            send(k[1], self.columns(near), here, dev(zl_=other, zh_=near))
            send(k[0], self.columns(zh), here, pair)
            self.own = local(self.columns(zh), here)

        def scatter_rest(self):
            k, here = self.k, self.buf.at[zh, y, half(zl)]
            send(k[3], self.columns(opp), here, dev(zl_=other, zh_=opp))
            send(k[3], self.columns(opp), here, dev(zh_=opp))

        def own_ready(self):
            self.own.wait()
            arrived(self.k[0], self.buf.at[zh, y, half(other)])

        def near_ready(self):
            block = self.buf.at[near, y]
            arrived(self.k[1], block)
            send(self.k[2], block, block, pair)

        def far_ready(self):
            arrived(self.k[2], self.buf.at[far, y])

        def opp_ready(self):
            arrived(self.k[3], self.buf.at[opp, y])

    class Gather:
        def __init__(self, buf, ring, s):
            self.buf, self.ring, self.s = buf, ring, s
            self.k = [sem() for _ in range(3)]

        def at(self, block, rows=pl.ds(0, 64)):
            return self.buf.at[self.s, block, rows]

        def start(self):
            r, mine = self.ring, self.at(self.ring.me)
            send(self.k[0], mine, mine, r.plus)
            send(self.k[1], mine, mine, r.minus)

        def forward(self):
            r = self.ring
            arrived(self.k[0], self.at(r.m))
            send(self.k[2], self.at(r.m, LO), self.at(r.m, LO), r.plus)
            arrived(self.k[1], self.at(r.p))
            send(self.k[2], self.at(r.p, HI), self.at(r.p, HI), r.minus)

        def done(self):
            r = self.ring
            arrived(self.k[2], self.at(r.o))

    class Scatter:
        def __init__(self, part, first, second, mixed, ring, t):
            self.part, self.first, self.second, self.mixed = (
                part.at[t], first.at[t], second.at[t], mixed.at[t]
            )
            self.ring = ring
            self.k = [sem() for _ in range(3)]

        def start(self):
            r, k = self.ring, self.k
            send(k[0], self.part.at[r.o, LO], self.first.at[0], r.plus)
            send(k[1], self.part.at[r.o, HI], self.first.at[1], r.minus)
            send(k[2], self.part.at[r.p, HI], self.second.at[0, HI], r.plus)
            send(k[2], self.part.at[r.m, LO], self.second.at[1, LO], r.minus)

        def middle(self):
            r, k = self.ring, self.k
            for way, rows, block, to in ((0, LO, r.p, r.plus), (1, HI, r.m, r.minus)):
                arrived(k[way], self.first.at[way])
                total = self.part[block, rows].astype(F32) + self.first[way].astype(F32)
                self.mixed[way] = total.astype(BF)
                send(k[2], self.mixed.at[way], self.second.at[way, rows], to)

        def end(self):
            arrived(self.k[2], self.second)
            return (
                self.part[self.ring.me].astype(F32)
                + self.second[0].astype(F32)
                + self.second[1].astype(F32)
            )

    class Depth:
        def __init__(self, buf):
            self.buf = buf
            self.k = [sem() for _ in range(3)]

        def start(self):
            mine = self.buf.at[zh, x]
            send(self.k[0], mine, mine, dev(zh_=up))
            send(self.k[1], mine, mine, dev(zh_=down))

        def here(self):
            arrived(self.k[0], self.buf.at[down, x])
            arrived(self.k[1], self.buf.at[up, x])

        def send_on(self):
            for came, rows, to in ((down, LO, up), (up, HI, down)):
                piece = self.buf.at[came, x, rows]
                send(self.k[2], piece, piece, dev(zh_=to))

        def done(self):
            arrived(self.k[2], self.buf.at[opp, x])

    rows_g, rows_a = Rows(grad, G), Rows(acts, A)
    g_y = [Gather(G, ry, s) for s in order]
    a_y = [Gather(A, ry, s) for s in order]
    c_z, c_x = Depth(AC), [Gather(AC, rx, s) for s in order]
    h_x = [Scatter(HP, H1, H2, HX, rx, t) for t in range(4)]
    h_k = sem()
    d_z, d_x = Depth(D), [Gather(D, rx, s) for s in ring]
    q_y = [Scatter(QP, Q1, Q2, QX, ry, t) for t in range(4)]
    q_k = [sem() for _ in range(4)]
    i_k = [sem() for _ in range(3)]
    w_k = [sem() for _ in range(2)]
    g_k = [sem() for _ in range(2)]
    b_k = sem()
    OWN, NEAR, FAR, OPP = range(4)
    UP, DOWN = 1, 2

    mine = pl.ds(pl.multiple_of(core * 448, 448), 448)
    theirs = pl.ds(pl.multiple_of((1 - core) * 448, 448), 448)
    own_w = [None, None]

    def weights(i, src, buf):
        send(w_k[i], src, buf.at[mine], twin)
        own_w[i] = local(src, buf.at[mine])

    def activations():
        staged[1].wait()
        value, slope = gelu_parts(pre[...].astype(F32))
        AC[zh, x] = value.astype(BF)
        SL[...] = slope

    def entry():
        pl.semaphore_wait(barrier, len(peers))
        staged[0].wait()

    def hidden(t, first=False):
        g_y[t].done()
        if first:
            own_w[0].wait()
            arrived(w_k[0], WO.at[theirs])
        part = dot(G[order[t]].reshape(256, W), WO[...], ((1,), (0,)))
        HP[t] = part.astype(BF).reshape(4, 64, W)
        h_x[t].start()

    def hidden_end(t):
        total = h_x[t].end()
        if t == OWN:
            HS[...] = total
        else:
            HB[t - 1] = total.astype(BF)
            send(h_k, HB.at[t - 1], ZR.at[t - 1], dev(zh_=order[t]))

    def dh_rows():
        total = HS[...]
        arrived(h_k, ZR)
        for t in range(3):
            total = total + ZR[t].astype(F32)
        D[zh, x] = (total * SL[...]).astype(BF)

    def weight_grad(i, t, first=False):
        rows, cols = ((A, D), (G, AC))[i]
        s = ring[t] if i == 0 else order[t]
        right = cols[s].reshape(256, W)
        for low, size in ((0, 512), (512, 384)):
            left = rows[s, :, :, low : low + size].reshape(256, size)
            term = dot(left, right, ((0,), (0,)))
            if first:
                ACC[i, low : low + size] = term
            else:
                ACC[i, low : low + size] += term

    def share(i):
        WS[i] = ACC[i, theirs].astype(BF)
        send(g_k[i], WS.at[i], WR.at[i], twin)

    def inputs(t, first=False):
        d_x[t].done()
        if first:
            own_w[1].wait()
            arrived(w_k[1], WI.at[theirs])
        part = dot(D[ring[t]].reshape(256, W), WI[...], ((1,), (1,)))
        QP[t] = part.astype(BF).reshape(4, 64, W)
        q_y[t].start()

    def inputs_end(t):
        QS[t] = q_y[t].end()
        ZS[t] = QS[t, half(other)].astype(BF)
        send(q_k[t], ZS.at[t], ZL.at[t], pair)

    def inputs_out(t):
        arrived(q_k[t], ZL.at[t])
        total = (QS[t, half(zl)] + ZL[t].astype(F32)).astype(BF)
        if t == OWN:
            IR[zh] = total
        else:
            IS[t] = total
            send(i_k[t - 1], IS.at[t], IR.at[zh], dev(zh_=ring[t]))

    def bias_sums():
        BS[...] = jnp.sum(D[...].astype(F32).reshape(128, 8, W), axis=0)
        send(b_k, BS, BR, twin)

    def finish_bias():
        arrived(b_k, BR)
        o_bias[...] = jnp.sum(BS[...] + BR[...], axis=0)

    def finish_weight(i, out):
        arrived(g_k[i], WR.at[i])
        out[...] = (ACC[i, mine] + WR[i].astype(F32)).astype(BF)

    def finish_inputs():
        for t in range(1, 4):
            arrived(i_k[(None, 1, 0, 2)[t]], IR.at[ring[t]])
        for k in range(4):
            o_ig[:, k * W : (k + 1) * W] = IR[k]

    def finish_sends():
        for copy in sends[-N_SENDS:]:
            copy.wait_send()

    activations()
    entry()
    rows_g.scatter()
    weights(0, w_out, WO)
    rows_g.near_ready()
    g_y[NEAR].start()
    rows_g.scatter_rest()
    c_x[OWN].start()
    rows_g.own_ready()
    g_y[NEAR].forward()
    rows_g.far_ready()
    g_y[FAR].start()
    hidden(NEAR, True)
    rows_g.opp_ready()
    g_y[OPP].start()
    c_z.start()
    g_y[FAR].forward()
    staged[2].wait()
    rows_a.scatter()
    rows_a.scatter_rest()
    h_x[NEAR].middle()
    g_y[OWN].start()
    g_y[OPP].forward()
    hidden(FAR)
    c_x[OWN].forward()
    g_y[OWN].forward()
    hidden(OPP)
    rows_a.near_ready()
    h_x[FAR].middle()
    hidden_end(NEAR)
    hidden(OWN)
    h_x[OPP].middle()
    a_y[NEAR].start()
    hidden_end(FAR)
    h_x[OWN].middle()
    hidden_end(OPP)
    weights(1, w_in, WI)
    hidden_end(OWN)
    c_z.here()
    c_x[NEAR].start()
    rows_a.far_ready()
    a_y[FAR].start()
    rows_a.opp_ready()
    a_y[NEAR].forward()
    a_y[OPP].start()
    c_x[OWN].done()
    weight_grad(1, OWN, True)
    c_x[FAR].start()
    rows_a.own_ready()
    dh_rows()
    d_x[OWN].start()
    d_z.start()
    a_y[FAR].forward()
    a_y[OWN].start()
    d_x[OWN].forward()
    a_y[OPP].forward()
    d_z.here()
    d_x[UP].start()
    d_z.send_on()
    inputs(OWN, True)
    a_y[OWN].forward()
    d_x[DOWN].start()
    c_z.send_on()
    d_x[UP].forward()
    d_z.done()
    d_x[OPP].start()
    q_y[OWN].middle()
    d_x[DOWN].forward()
    inputs(UP)
    inputs_end(OWN)
    d_x[OPP].forward()
    c_x[NEAR].forward()
    c_x[FAR].forward()
    c_z.done()
    c_x[OPP].start()
    inputs(DOWN)
    q_y[UP].middle()
    inputs_out(OWN)
    for t in range(4):
        a_y[t].done()
    weight_grad(0, OWN, True)
    weight_grad(0, UP)
    inputs(OPP)
    q_y[DOWN].middle()
    inputs_end(UP)
    weight_grad(0, DOWN)
    weight_grad(0, OPP)
    share(0)
    q_y[OPP].middle()
    inputs_end(DOWN)
    bias_sums()
    c_x[OPP].forward()
    c_x[NEAR].done()
    weight_grad(1, NEAR)
    inputs_end(OPP)
    inputs_out(UP)
    c_x[FAR].done()
    weight_grad(1, FAR)
    inputs_out(DOWN)
    c_x[OPP].done()
    weight_grad(1, OPP)
    share(1)
    inputs_out(OPP)
    finish_weight(0, o_iw)
    finish_bias()
    finish_weight(1, o_ow)
    finish_inputs()
    finish_sends()


def deliver(from_ig, from_iw, from_ow, from_bias, o_ig, o_iw, o_ow, o_bias, sem):
    pieces = [(from_bias, o_bias)]
    for src, dst, rows in ((from_iw, o_iw, 224), (from_ow, o_ow, 224), (from_ig, o_ig, 16)):
        for k in range(src.shape[0] // rows):
            at = pl.ds(k * rows, rows)
            pieces.append((src.at[at], dst.at[at]))
    copies = [pltpu.make_async_copy(a, b, sem.at[k]) for k, (a, b) in enumerate(pieces)]
    for copy in copies:
        copy.start()
    for copy in copies:
        copy.wait()


def shards(acts, preact, out_grad, w_in, w_out):
    vmem = pl.BlockSpec(memory_space=pltpu.VMEM)
    bf = lambda *shape: pltpu.VMEM(shape, BF)
    f32 = lambda *shape: pltpu.VMEM(shape, F32)
    scratch = dict(
        acts=bf(32, 4 * W), pre=bf(64, W), grad=bf(32, 4 * W),
        G=bf(4, 4, 64, W), A=bf(4, 4, 64, W), AC=bf(4, 4, 64, W), D=bf(4, 4, 64, W),
        WO=bf(W, W), WI=bf(W, W),
        HP=bf(4, 4, 64, W), H1=bf(4, 2, 32, W), H2=bf(4, 2, 64, W), HX=bf(4, 2, 32, W),
        HS=f32(64, W), HB=bf(3, 64, W), ZR=bf(3, 64, W), SL=f32(64, W),
        QP=bf(4, 4, 64, W), Q1=bf(4, 2, 32, W), Q2=bf(4, 2, 64, W), QX=bf(4, 2, 32, W),
        QS=f32(4, 64, W), ZS=bf(4, 32, W), ZL=bf(4, 32, W), IS=bf(4, 32, W), IR=bf(4, 32, W),
        ACC=f32(2, W, W), WS=bf(2, 448, W), WR=bf(2, 448, W),
        BS=f32(8, W), BR=f32(8, W),
        send_sem=pltpu.SemaphoreType.DMA((N_SENDS,)),
        recv_sem=pltpu.SemaphoreType.DMA((N_SEMS,)),
        local_sem=pltpu.SemaphoreType.DMA((16,)),
    )
    hbm = pl.BlockSpec(memory_space=pl.ANY)
    parts = pl.pallas_call(
        kernel,
        out_shape=(bf(32, 4 * W), bf(448, W), bf(448, W), f32(W)),
        in_specs=[hbm] * 5,
        out_specs=[vmem] * 4,
        scratch_shapes=list(scratch.values()),
        compiler_params=pltpu.CompilerParams(
            collective_id=0, has_side_effects=True, vmem_limit_bytes=60 * 2**20
        ),
    )(acts, preact, out_grad, w_in, w_out)
    return pl.pallas_call(
        deliver,
        out_shape=tuple(jax.ShapeDtypeStruct(p.shape, p.dtype) for p in parts),
        in_specs=[vmem] * 4,
        out_specs=[hbm] * 4,
        scratch_shapes=[pltpu.SemaphoreType.DMA((7,))],
        compiler_params=pltpu.CompilerParams(vmem_limit_bytes=2**20),
    )(*parts)


def solution(mesh):
    return jax.shard_map(
        shards,
        mesh=mesh,
        in_specs=(
            P(("gz", "gy"), "gx"),
            P(("gz", "gx"), "gy"),
            P(("gz", "gy"), "gx"),
            P(("gx", "gz"), "gy"),
            P(("gx", "gz"), "gy"),
        ),
        out_specs=(P(("gz", "gy"), "gx"), P(("gx", "gz"), "gy"), P(("gx", "gz"), "gy"), P("gy")),
        check_vma=False,
    )
```

```python
import jax
import jax.numpy as jnp
from jax import lax
from jax.experimental import pallas as pl
from jax.experimental.pallas import tpu as pltpu
from jax.sharding import PartitionSpec as P

MESH = pl.DeviceIdType.MESH
BF = jnp.bfloat16
F32 = jnp.float32
W = 896
N_SEMS = 100
N_SENDS = 32


def gelu_parts(pre):
    coeff = 0.7978845608028654
    inner = coeff * (pre + 0.044715 * pre * pre * pre)
    tangent = jnp.tanh(inner)
    value = 0.5 * pre * (1.0 + tangent)
    slope = 0.5 * (1.0 + tangent) + 0.5 * pre * (1.0 - tangent * tangent) * coeff * (
        1.0 + 3.0 * 0.044715 * pre * pre
    )
    return (value, slope)


def dot(left, right, dims):
    return lax.dot_general(left, right, (dims, ((), ())), preferred_element_type=F32)


class Ring:
    def __init__(self, me, device):
        self.me = me
        self.p, self.m, self.o = (lax.rem(me + k, 4) for k in (1, 3, 2))
        self.plus, self.minus = device(self.p), device(self.m)


def kernel(
    acts_hbm, pre_hbm, grad_hbm, w_in, w_out,
    o_ig, o_iw, o_ow, o_bias,
    acts, pre, grad,
    G, A, AC, D, WO, WI,
    HP, H1, H2, HX, HS, HB, ZR, SL,
    QP, Q1, Q2, QX, QS, ZS, ZL, IS, IR,
    ACC, WS, WR, BS, BR,
    send_sem, recv_sem, local_sem,
):
    gx, gy, gz = (lax.axis_index(name) for name in ("gx", "gy", "gz"))
    y, zl = gy // 2, lax.rem(gy, 2)
    zh, core = gz // 2, lax.rem(gz, 2)
    x = gx
    other = 1 - zl

    def dev(x_=x, y_=y, zl_=zl, zh_=zh, c_=core):
        return (x_, y_ * 2 + zl_, zh_ * 2 + c_)

    up, down, opp = (lax.rem(zh + k, 4) for k in (1, 3, 2))
    near = jnp.where(zl == 0, down, up)
    far = jnp.where(zl == 0, up, down)
    order = (zh, near, far, opp)
    ring = (zh, up, down, opp)
    twin = dev(c_=1 - core)
    pair = dev(zl_=other)
    rx = Ring(x, lambda k: dev(x_=k))
    ry = Ring(y, lambda k: dev(y_=k))

    peers = [rx.plus, rx.minus, ry.plus, ry.minus, twin, pair]
    peers += [dev(zh_=k) for k in (up, down, opp)]
    peers += [dev(zl_=other, zh_=near), dev(zl_=other, zh_=opp)]
    barrier = pltpu.get_barrier_semaphore()
    for peer in peers:
        pl.semaphore_signal(barrier, inc=1, device_id=peer, device_id_type=MESH)

    count = [0]
    sends = []

    def sem():
        count[0] += 1
        return count[0] - 1

    def send(k, src, dst, to):
        n = len(sends)
        if n >= N_SENDS:
            sends[n - N_SENDS].wait_send()
        copy = pltpu.make_async_remote_copy(
            src_ref=src, dst_ref=dst, send_sem=send_sem.at[n % N_SENDS], recv_sem=recv_sem.at[k],
            device_id=to, device_id_type=MESH,
        )
        copy.start()
        sends.append(copy)

    def arrived(k, dst):
        pltpu.make_async_remote_copy(
            src_ref=dst, dst_ref=dst, send_sem=send_sem.at[0], recv_sem=recv_sem.at[k],
            device_id=twin, device_id_type=MESH,
        ).wait_recv()

    n_local = [0]

    def local(src, dst):
        copy = pltpu.make_async_copy(src, dst, local_sem.at[n_local[0]])
        n_local[0] += 1
        copy.start()
        return copy

    staged = [local(a, b) for a, b in ((grad_hbm, grad), (pre_hbm, pre), (acts_hbm, acts))]

    def half(k):
        return pl.ds(pl.multiple_of(k * 32, 32), 32)

    LO, HI = pl.ds(0, 32), pl.ds(32, 32)

    class Rows:
        def __init__(self, src, buf):
            self.src, self.buf = src, buf
            self.k = [sem() for _ in range(4)]

        def columns(self, k):
            return self.src.at[:, pl.ds(pl.multiple_of(k * W, W), W)]

        def scatter(self):
            k, here = self.k, self.buf.at[zh, y, half(zl)]
            send(k[1], self.columns(far), here, dev(zh_=far))
            send(k[1], self.columns(near), here, dev(zl_=other, zh_=near))
            send(k[0], self.columns(zh), here, pair)
            self.own = local(self.columns(zh), here)

        def scatter_rest(self):
            k, here = self.k, self.buf.at[zh, y, half(zl)]
            send(k[3], self.columns(opp), here, dev(zl_=other, zh_=opp))
            send(k[3], self.columns(opp), here, dev(zh_=opp))

        def own_ready(self):
            self.own.wait()
            arrived(self.k[0], self.buf.at[zh, y, half(other)])

        def near_ready(self):
            block = self.buf.at[near, y]
            arrived(self.k[1], block)
            send(self.k[2], block, block, pair)

        def far_ready(self):
            arrived(self.k[2], self.buf.at[far, y])

        def opp_ready(self):
            arrived(self.k[3], self.buf.at[opp, y])

    class Gather:
        def __init__(self, buf, ring, s):
            self.buf, self.ring, self.s = buf, ring, s
            self.k = [sem() for _ in range(3)]

        def at(self, block, rows=pl.ds(0, 64)):
            return self.buf.at[self.s, block, rows]

        def start(self):
            r, mine = self.ring, self.at(self.ring.me)
            send(self.k[0], mine, mine, r.plus)
            send(self.k[1], mine, mine, r.minus)

        def forward(self):
            r = self.ring
            arrived(self.k[0], self.at(r.m))
            send(self.k[2], self.at(r.m, LO), self.at(r.m, LO), r.plus)
            arrived(self.k[1], self.at(r.p))
            send(self.k[2], self.at(r.p, HI), self.at(r.p, HI), r.minus)

        def done(self):
            r = self.ring
            arrived(self.k[2], self.at(r.o))

    class Scatter:
        def __init__(self, part, first, second, mixed, ring, t):
            self.part, self.first, self.second, self.mixed = (
                part.at[t], first.at[t], second.at[t], mixed.at[t]
            )
            self.ring = ring
            self.k = [sem() for _ in range(3)]

        def start(self):
            r, k = self.ring, self.k
            send(k[0], self.part.at[r.o, LO], self.first.at[0], r.plus)
            send(k[1], self.part.at[r.o, HI], self.first.at[1], r.minus)
            send(k[2], self.part.at[r.p, HI], self.second.at[0, HI], r.plus)
            send(k[2], self.part.at[r.m, LO], self.second.at[1, LO], r.minus)

        def middle(self):
            r, k = self.ring, self.k
            for way, rows, block, to in ((0, LO, r.p, r.plus), (1, HI, r.m, r.minus)):
                arrived(k[way], self.first.at[way])
                total = self.part[block, rows].astype(F32) + self.first[way].astype(F32)
                self.mixed[way] = total.astype(BF)
                send(k[2], self.mixed.at[way], self.second.at[way, rows], to)

        def end(self):
            arrived(self.k[2], self.second)
            return (
                self.part[self.ring.me].astype(F32)
                + self.second[0].astype(F32)
                + self.second[1].astype(F32)
            )

    class Depth:
        def __init__(self, buf):
            self.buf = buf
            self.k = [sem() for _ in range(3)]

        def start(self):
            mine = self.buf.at[zh, x]
            send(self.k[0], mine, mine, dev(zh_=up))
            send(self.k[1], mine, mine, dev(zh_=down))

        def here(self):
            arrived(self.k[0], self.buf.at[down, x])
            arrived(self.k[1], self.buf.at[up, x])

        def send_on(self):
            for came, rows, to in ((down, LO, up), (up, HI, down)):
                piece = self.buf.at[came, x, rows]
                send(self.k[2], piece, piece, dev(zh_=to))

        def done(self):
            arrived(self.k[2], self.buf.at[opp, x])

    rows_g, rows_a = Rows(grad, G), Rows(acts, A)
    g_y = [Gather(G, ry, s) for s in order]
    a_y = [Gather(A, ry, s) for s in order]
    c_z, c_x = Depth(AC), [Gather(AC, rx, s) for s in order]
    h_x = [Scatter(HP, H1, H2, HX, rx, t) for t in range(4)]
    h_k = sem()
    d_z, d_x = Depth(D), [Gather(D, rx, s) for s in ring]
    q_y = [Scatter(QP, Q1, Q2, QX, ry, t) for t in range(4)]
    q_k = [sem() for _ in range(4)]
    i_k = [sem() for _ in range(3)]
    w_k = [sem() for _ in range(2)]
    g_k = [sem() for _ in range(2)]
    b_k = sem()
    OWN, NEAR, FAR, OPP = range(4)
    UP, DOWN = 1, 2

    mine = pl.ds(pl.multiple_of(core * 448, 448), 448)
    theirs = pl.ds(pl.multiple_of((1 - core) * 448, 448), 448)
    own_w = [None, None]

    def weights(i, src, buf):
        send(w_k[i], src, buf.at[mine], twin)
        own_w[i] = local(src, buf.at[mine])

    def activations():
        staged[1].wait()
        value, slope = gelu_parts(pre[...].astype(F32))
        AC[zh, x] = value.astype(BF)
        SL[...] = slope

    def entry():
        pl.semaphore_wait(barrier, len(peers))
        staged[0].wait()

    def hidden(t, first=False):
        g_y[t].done()
        if first:
            own_w[0].wait()
            arrived(w_k[0], WO.at[theirs])
        part = dot(G[order[t]].reshape(256, W), WO[...], ((1,), (0,)))
        HP[t] = part.astype(BF).reshape(4, 64, W)
        h_x[t].start()

    def hidden_end(t):
        total = h_x[t].end()
        if t == OWN:
            HS[...] = total
        else:
            HB[t - 1] = total.astype(BF)
            send(h_k, HB.at[t - 1], ZR.at[t - 1], dev(zh_=order[t]))

    def dh_rows():
        total = HS[...]
        arrived(h_k, ZR)
        for t in range(3):
            total = total + ZR[t].astype(F32)
        D[zh, x] = (total * SL[...]).astype(BF)

    def weight_grad(i, t, first=False):
        rows, cols = ((A, D), (G, AC))[i]
        s = ring[t] if i == 0 else order[t]
        right = cols[s].reshape(256, W)
        for low, size in ((0, 512), (512, 384)):
            left = rows[s, :, :, low : low + size].reshape(256, size)
            term = dot(left, right, ((0,), (0,)))
            if first:
                ACC[i, low : low + size] = term
            else:
                ACC[i, low : low + size] += term

    def share(i):
        WS[i] = ACC[i, theirs].astype(BF)
        send(g_k[i], WS.at[i], WR.at[i], twin)

    def inputs(t, first=False):
        d_x[t].done()
        if first:
            own_w[1].wait()
            arrived(w_k[1], WI.at[theirs])
        part = dot(D[ring[t]].reshape(256, W), WI[...], ((1,), (1,)))
        QP[t] = part.astype(BF).reshape(4, 64, W)
        q_y[t].start()

    def inputs_end(t):
        QS[t] = q_y[t].end()
        ZS[t] = QS[t, half(other)].astype(BF)
        send(q_k[t], ZS.at[t], ZL.at[t], pair)

    def inputs_out(t):
        arrived(q_k[t], ZL.at[t])
        total = (QS[t, half(zl)] + ZL[t].astype(F32)).astype(BF)
        if t == OWN:
            IR[zh] = total
        else:
            IS[t] = total
            send(i_k[t - 1], IS.at[t], IR.at[zh], dev(zh_=ring[t]))

    def bias_sums():
        BS[...] = jnp.sum(D[...].astype(F32).reshape(128, 8, W), axis=0)
        send(b_k, BS, BR, twin)

    def finish_bias():
        arrived(b_k, BR)
        o_bias[...] = jnp.sum(BS[...] + BR[...], axis=0)

    def finish_weight(i, out):
        arrived(g_k[i], WR.at[i])
        out[...] = (ACC[i, mine] + WR[i].astype(F32)).astype(BF)

    def finish_inputs():
        for t in range(1, 4):
            arrived(i_k[(None, 1, 0, 2)[t]], IR.at[ring[t]])
        for k in range(4):
            o_ig[:, k * W : (k + 1) * W] = IR[k]

    def finish_sends():
        for copy in sends[-N_SENDS:]:
            copy.wait_send()

    activations()
    entry()
    rows_g.scatter()
    weights(0, w_out, WO)
    rows_g.near_ready()
    g_y[NEAR].start()
    rows_g.scatter_rest()
    c_x[OWN].start()
    rows_g.own_ready()
    g_y[NEAR].forward()
    rows_g.far_ready()
    g_y[FAR].start()
    hidden(NEAR, True)
    rows_g.opp_ready()
    g_y[OPP].start()
    c_z.start()
    g_y[FAR].forward()
    staged[2].wait()
    rows_a.scatter()
    rows_a.scatter_rest()
    h_x[NEAR].middle()
    g_y[OWN].start()
    g_y[OPP].forward()
    hidden(FAR)
    c_x[OWN].forward()
    g_y[OWN].forward()
    hidden(OPP)
    rows_a.near_ready()
    h_x[FAR].middle()
    hidden_end(NEAR)
    hidden(OWN)
    h_x[OPP].middle()
    a_y[NEAR].start()
    hidden_end(FAR)
    h_x[OWN].middle()
    hidden_end(OPP)
    weights(1, w_in, WI)
    hidden_end(OWN)
    c_z.here()
    c_x[NEAR].start()
    rows_a.far_ready()
    a_y[FAR].start()
    rows_a.opp_ready()
    a_y[NEAR].forward()
    a_y[OPP].start()
    c_x[OWN].done()
    weight_grad(1, OWN, True)
    c_x[FAR].start()
    rows_a.own_ready()
    dh_rows()
    d_x[OWN].start()
    d_z.start()
    a_y[FAR].forward()
    a_y[OWN].start()
    d_x[OWN].forward()
    a_y[OPP].forward()
    d_z.here()
    d_x[UP].start()
    d_z.send_on()
    inputs(OWN, True)
    a_y[OWN].forward()
    d_x[DOWN].start()
    c_z.send_on()
    d_x[UP].forward()
    d_z.done()
    d_x[OPP].start()
    q_y[OWN].middle()
    d_x[DOWN].forward()
    inputs(UP)
    inputs_end(OWN)
    d_x[OPP].forward()
    c_x[NEAR].forward()
    c_x[FAR].forward()
    c_z.done()
    c_x[OPP].start()
    inputs(DOWN)
    q_y[UP].middle()
    inputs_out(OWN)
    for t in range(4):
        a_y[t].done()
    weight_grad(0, OWN, True)
    weight_grad(0, UP)
    inputs(OPP)
    q_y[DOWN].middle()
    inputs_end(UP)
    c_x[OPP].forward()
    weight_grad(0, DOWN)
    weight_grad(0, OPP)
    share(0)
    q_y[OPP].middle()
    inputs_end(DOWN)
    bias_sums()
    c_x[NEAR].done()
    weight_grad(1, NEAR)
    c_x[FAR].done()
    weight_grad(1, FAR)
    c_x[OPP].done()
    weight_grad(1, OPP)
    share(1)
    inputs_end(OPP)
    inputs_out(UP)
    inputs_out(DOWN)
    inputs_out(OPP)
    finish_weight(0, o_iw)
    finish_bias()
    finish_weight(1, o_ow)
    finish_inputs()
    finish_sends()


def deliver(from_ig, from_iw, from_ow, from_bias, o_ig, o_iw, o_ow, o_bias, sem):
    pieces = [(from_bias, o_bias)]
    for src, dst, rows in ((from_iw, o_iw, 224), (from_ow, o_ow, 224), (from_ig, o_ig, 16)):
        for k in range(src.shape[0] // rows):
            at = pl.ds(k * rows, rows)
            pieces.append((src.at[at], dst.at[at]))
    copies = [pltpu.make_async_copy(a, b, sem.at[k]) for k, (a, b) in enumerate(pieces)]
    for copy in copies:
        copy.start()
    for copy in copies:
        copy.wait()


def shards(acts, preact, out_grad, w_in, w_out):
    vmem = pl.BlockSpec(memory_space=pltpu.VMEM)
    bf = lambda *shape: pltpu.VMEM(shape, BF)
    f32 = lambda *shape: pltpu.VMEM(shape, F32)
    scratch = dict(
        acts=bf(32, 4 * W), pre=bf(64, W), grad=bf(32, 4 * W),
        G=bf(4, 4, 64, W), A=bf(4, 4, 64, W), AC=bf(4, 4, 64, W), D=bf(4, 4, 64, W),
        WO=bf(W, W), WI=bf(W, W),
        HP=bf(4, 4, 64, W), H1=bf(4, 2, 32, W), H2=bf(4, 2, 64, W), HX=bf(4, 2, 32, W),
        HS=f32(64, W), HB=bf(3, 64, W), ZR=bf(3, 64, W), SL=f32(64, W),
        QP=bf(4, 4, 64, W), Q1=bf(4, 2, 32, W), Q2=bf(4, 2, 64, W), QX=bf(4, 2, 32, W),
        QS=f32(4, 64, W), ZS=bf(4, 32, W), ZL=bf(4, 32, W), IS=bf(4, 32, W), IR=bf(4, 32, W),
        ACC=f32(2, W, W), WS=bf(2, 448, W), WR=bf(2, 448, W),
        BS=f32(8, W), BR=f32(8, W),
        send_sem=pltpu.SemaphoreType.DMA((N_SENDS,)),
        recv_sem=pltpu.SemaphoreType.DMA((N_SEMS,)),
        local_sem=pltpu.SemaphoreType.DMA((16,)),
    )
    hbm = pl.BlockSpec(memory_space=pl.ANY)
    parts = pl.pallas_call(
        kernel,
        out_shape=(bf(32, 4 * W), bf(448, W), bf(448, W), f32(W)),
        in_specs=[hbm] * 5,
        out_specs=[vmem] * 4,
        scratch_shapes=list(scratch.values()),
        compiler_params=pltpu.CompilerParams(
            collective_id=0, has_side_effects=True, vmem_limit_bytes=60 * 2**20
        ),
    )(acts, preact, out_grad, w_in, w_out)
    return pl.pallas_call(
        deliver,
        out_shape=tuple(jax.ShapeDtypeStruct(p.shape, p.dtype) for p in parts),
        in_specs=[vmem] * 4,
        out_specs=[hbm] * 4,
        scratch_shapes=[pltpu.SemaphoreType.DMA((7,))],
        compiler_params=pltpu.CompilerParams(vmem_limit_bytes=2**20),
    )(*parts)


def solution(mesh):
    return jax.shard_map(
        shards,
        mesh=mesh,
        in_specs=(
            P(("gz", "gy"), "gx"),
            P(("gz", "gx"), "gy"),
            P(("gz", "gy"), "gx"),
            P(("gx", "gz"), "gy"),
            P(("gx", "gz"), "gy"),
        ),
        out_specs=(P(("gz", "gy"), "gx"), P(("gx", "gz"), "gy"), P(("gx", "gz"), "gy"), P("gy")),
        check_vma=False,
    )
```

```python
import jax
import jax.numpy as jnp
from jax import lax
from jax.experimental import pallas as pl
from jax.experimental.pallas import tpu as pltpu
from jax.sharding import PartitionSpec as P

MESH = pl.DeviceIdType.MESH
BF = jnp.bfloat16
F32 = jnp.float32
W = 896
N_SEMS = 100
N_SENDS = 32


def gelu_parts(pre):
    coeff = 0.7978845608028654
    inner = coeff * (pre + 0.044715 * pre * pre * pre)
    tangent = jnp.tanh(inner)
    value = 0.5 * pre * (1.0 + tangent)
    slope = 0.5 * (1.0 + tangent) + 0.5 * pre * (1.0 - tangent * tangent) * coeff * (
        1.0 + 3.0 * 0.044715 * pre * pre
    )
    return (value, slope)


def dot(left, right, dims):
    return lax.dot_general(left, right, (dims, ((), ())), preferred_element_type=F32)


class Ring:
    def __init__(self, me, device):
        self.me = me
        self.p, self.m, self.o = (lax.rem(me + k, 4) for k in (1, 3, 2))
        self.plus, self.minus = device(self.p), device(self.m)


def kernel(
    acts_hbm, pre_hbm, grad_hbm, w_in, w_out,
    o_ig, o_iw, o_ow, o_bias,
    acts, pre, grad,
    G, A, AC, D, WO, WI,
    HP, H1, H2, HX, HS, HB, ZR, SL,
    QP, Q1, Q2, QX, QS, ZS, ZL, IS, IR,
    ACC, WS, WR, BS, BR,
    send_sem, recv_sem, local_sem,
):
    gx, gy, gz = (lax.axis_index(name) for name in ("gx", "gy", "gz"))
    y, zl = gy // 2, lax.rem(gy, 2)
    zh, core = gz // 2, lax.rem(gz, 2)
    x = gx
    other = 1 - zl

    def dev(x_=x, y_=y, zl_=zl, zh_=zh, c_=core):
        return (x_, y_ * 2 + zl_, zh_ * 2 + c_)

    up, down, opp = (lax.rem(zh + k, 4) for k in (1, 3, 2))
    near = jnp.where(zl == 0, down, up)
    far = jnp.where(zl == 0, up, down)
    order = (zh, near, far, opp)
    ring = (zh, up, down, opp)
    twin = dev(c_=1 - core)
    pair = dev(zl_=other)
    rx = Ring(x, lambda k: dev(x_=k))
    ry = Ring(y, lambda k: dev(y_=k))

    peers = [rx.plus, rx.minus, ry.plus, ry.minus, twin, pair]
    peers += [dev(zh_=k) for k in (up, down, opp)]
    peers += [dev(zl_=other, zh_=near), dev(zl_=other, zh_=opp)]
    barrier = pltpu.get_barrier_semaphore()
    for peer in peers:
        pl.semaphore_signal(barrier, inc=1, device_id=peer, device_id_type=MESH)

    count = [0]
    sends = []

    def sem():
        count[0] += 1
        return count[0] - 1

    def send(k, src, dst, to):
        n = len(sends)
        if n >= N_SENDS:
            sends[n - N_SENDS].wait_send()
        copy = pltpu.make_async_remote_copy(
            src_ref=src, dst_ref=dst, send_sem=send_sem.at[n % N_SENDS], recv_sem=recv_sem.at[k],
            device_id=to, device_id_type=MESH,
        )
        copy.start()
        sends.append(copy)

    def arrived(k, dst):
        pltpu.make_async_remote_copy(
            src_ref=dst, dst_ref=dst, send_sem=send_sem.at[0], recv_sem=recv_sem.at[k],
            device_id=twin, device_id_type=MESH,
        ).wait_recv()

    n_local = [0]

    def local(src, dst):
        copy = pltpu.make_async_copy(src, dst, local_sem.at[n_local[0]])
        n_local[0] += 1
        copy.start()
        return copy

    staged = [local(a, b) for a, b in ((grad_hbm, grad), (pre_hbm, pre), (acts_hbm, acts))]

    def half(k):
        return pl.ds(pl.multiple_of(k * 32, 32), 32)

    LO, HI = pl.ds(0, 32), pl.ds(32, 32)

    class Rows:
        def __init__(self, src, buf):
            self.src, self.buf = src, buf
            self.k = [sem() for _ in range(4)]

        def columns(self, k):
            return self.src.at[:, pl.ds(pl.multiple_of(k * W, W), W)]

        def scatter(self):
            k, here = self.k, self.buf.at[zh, y, half(zl)]
            send(k[1], self.columns(far), here, dev(zh_=far))
            send(k[1], self.columns(near), here, dev(zl_=other, zh_=near))
            send(k[0], self.columns(zh), here, pair)
            self.own = local(self.columns(zh), here)

        def scatter_rest(self):
            k, here = self.k, self.buf.at[zh, y, half(zl)]
            send(k[3], self.columns(opp), here, dev(zl_=other, zh_=opp))
            send(k[3], self.columns(opp), here, dev(zh_=opp))

        def own_ready(self):
            self.own.wait()
            arrived(self.k[0], self.buf.at[zh, y, half(other)])

        def near_ready(self):
            block = self.buf.at[near, y]
            arrived(self.k[1], block)
            send(self.k[2], block, block, pair)

        def far_ready(self):
            arrived(self.k[2], self.buf.at[far, y])

        def opp_ready(self):
            arrived(self.k[3], self.buf.at[opp, y])

    class Gather:
        def __init__(self, buf, ring, s):
            self.buf, self.ring, self.s = buf, ring, s
            self.k = [sem() for _ in range(3)]

        def at(self, block, rows=pl.ds(0, 64)):
            return self.buf.at[self.s, block, rows]

        def start(self):
            r, mine = self.ring, self.at(self.ring.me)
            send(self.k[0], mine, mine, r.plus)
            send(self.k[1], mine, mine, r.minus)

        def forward(self):
            r = self.ring
            arrived(self.k[0], self.at(r.m))
            send(self.k[2], self.at(r.m, LO), self.at(r.m, LO), r.plus)
            arrived(self.k[1], self.at(r.p))
            send(self.k[2], self.at(r.p, HI), self.at(r.p, HI), r.minus)

        def done(self):
            r = self.ring
            arrived(self.k[2], self.at(r.o))

    class Scatter:
        def __init__(self, part, first, second, mixed, ring, t):
            self.part, self.first, self.second, self.mixed = (
                part.at[t], first.at[t], second.at[t], mixed.at[t]
            )
            self.ring = ring
            self.k = [sem() for _ in range(3)]

        def start(self):
            r, k = self.ring, self.k
            send(k[0], self.part.at[r.o, LO], self.first.at[0], r.plus)
            send(k[1], self.part.at[r.o, HI], self.first.at[1], r.minus)
            send(k[2], self.part.at[r.p, HI], self.second.at[0, HI], r.plus)
            send(k[2], self.part.at[r.m, LO], self.second.at[1, LO], r.minus)

        def middle(self):
            r, k = self.ring, self.k
            for way, rows, block, to in ((0, LO, r.p, r.plus), (1, HI, r.m, r.minus)):
                arrived(k[way], self.first.at[way])
                total = self.part[block, rows].astype(F32) + self.first[way].astype(F32)
                self.mixed[way] = total.astype(BF)
                send(k[2], self.mixed.at[way], self.second.at[way, rows], to)

        def end(self):
            arrived(self.k[2], self.second)
            return (
                self.part[self.ring.me].astype(F32)
                + self.second[0].astype(F32)
                + self.second[1].astype(F32)
            )

    class Depth:
        def __init__(self, buf):
            self.buf = buf
            self.k = [sem() for _ in range(3)]

        def start(self):
            mine = self.buf.at[zh, x]
            send(self.k[0], mine, mine, dev(zh_=up))
            send(self.k[1], mine, mine, dev(zh_=down))

        def here(self):
            arrived(self.k[0], self.buf.at[down, x])
            arrived(self.k[1], self.buf.at[up, x])

        def send_on(self):
            for came, rows, to in ((down, LO, up), (up, HI, down)):
                piece = self.buf.at[came, x, rows]
                send(self.k[2], piece, piece, dev(zh_=to))

        def done(self):
            arrived(self.k[2], self.buf.at[opp, x])

    rows_g, rows_a = Rows(grad, G), Rows(acts, A)
    g_y = [Gather(G, ry, s) for s in order]
    a_y = [Gather(A, ry, s) for s in order]
    c_z, c_x = Depth(AC), [Gather(AC, rx, s) for s in order]
    h_x = [Scatter(HP, H1, H2, HX, rx, t) for t in range(4)]
    h_k = sem()
    d_z, d_x = Depth(D), [Gather(D, rx, s) for s in ring]
    q_y = [Scatter(QP, Q1, Q2, QX, ry, t) for t in range(4)]
    q_k = [sem() for _ in range(4)]
    i_k = [sem() for _ in range(3)]
    w_k = [sem() for _ in range(2)]
    g_k = [sem() for _ in range(2)]
    b_k = sem()
    OWN, NEAR, FAR, OPP = range(4)
    UP, DOWN = 1, 2

    mine = pl.ds(pl.multiple_of(core * 448, 448), 448)
    theirs = pl.ds(pl.multiple_of((1 - core) * 448, 448), 448)
    own_w = [None, None]

    def weights(i, src, buf):
        send(w_k[i], src, buf.at[mine], twin)
        own_w[i] = local(src, buf.at[mine])

    def activations():
        staged[1].wait()
        value, slope = gelu_parts(pre[...].astype(F32))
        AC[zh, x] = value.astype(BF)
        SL[...] = slope

    def entry():
        pl.semaphore_wait(barrier, len(peers))
        staged[0].wait()

    def hidden(t, first=False):
        g_y[t].done()
        if first:
            own_w[0].wait()
            arrived(w_k[0], WO.at[theirs])
        part = dot(G[order[t]].reshape(256, W), WO[...], ((1,), (0,)))
        HP[t] = part.astype(BF).reshape(4, 64, W)
        h_x[t].start()

    def hidden_end(t):
        total = h_x[t].end()
        if t == OWN:
            HS[...] = total
        else:
            HB[t - 1] = total.astype(BF)
            send(h_k, HB.at[t - 1], ZR.at[t - 1], dev(zh_=order[t]))

    def dh_rows():
        total = HS[...]
        arrived(h_k, ZR)
        for t in range(3):
            total = total + ZR[t].astype(F32)
        D[zh, x] = (total * SL[...]).astype(BF)

    def weight_grad(i, t, first=False):
        rows, cols = ((A, D), (G, AC))[i]
        s = ring[t] if i == 0 else order[t]
        right = cols[s].reshape(256, W)
        for low, size in ((0, 512), (512, 384)):
            left = rows[s, :, :, low : low + size].reshape(256, size)
            term = dot(left, right, ((0,), (0,)))
            if first:
                ACC[i, low : low + size] = term
            else:
                ACC[i, low : low + size] += term

    def share(i):
        WS[i] = ACC[i, theirs].astype(BF)
        send(g_k[i], WS.at[i], WR.at[i], twin)

    def inputs(t, first=False):
        d_x[t].done()
        if first:
            own_w[1].wait()
            arrived(w_k[1], WI.at[theirs])
        part = dot(D[ring[t]].reshape(256, W), WI[...], ((1,), (1,)))
        QP[t] = part.astype(BF).reshape(4, 64, W)
        q_y[t].start()

    def inputs_end(t):
        QS[t] = q_y[t].end()
        ZS[t] = QS[t, half(other)].astype(BF)
        send(q_k[t], ZS.at[t], ZL.at[t], pair)

    def inputs_out(t):
        arrived(q_k[t], ZL.at[t])
        total = (QS[t, half(zl)] + ZL[t].astype(F32)).astype(BF)
        if t == OWN:
            IR[zh] = total
        else:
            IS[t] = total
            send(i_k[t - 1], IS.at[t], IR.at[zh], dev(zh_=ring[t]))

    def bias_sums():
        BS[...] = jnp.sum(D[...].astype(F32).reshape(128, 8, W), axis=0)
        send(b_k, BS, BR, twin)

    def finish_bias():
        arrived(b_k, BR)
        o_bias[...] = jnp.sum(BS[...] + BR[...], axis=0)

    def finish_weight(i, out):
        arrived(g_k[i], WR.at[i])
        out[...] = (ACC[i, mine] + WR[i].astype(F32)).astype(BF)

    def finish_inputs():
        for t in range(1, 4):
            arrived(i_k[(None, 1, 0, 2)[t]], IR.at[ring[t]])
        for k in range(4):
            o_ig[:, k * W : (k + 1) * W] = IR[k]

    def finish_sends():
        for copy in sends[-N_SENDS:]:
            copy.wait_send()

    entry()
    rows_g.scatter()
    weights(0, w_out, WO)
    activations()
    rows_g.near_ready()
    g_y[NEAR].start()
    rows_g.scatter_rest()
    c_x[OWN].start()
    rows_g.own_ready()
    g_y[NEAR].forward()
    rows_g.far_ready()
    g_y[FAR].start()
    hidden(NEAR, True)
    rows_g.opp_ready()
    g_y[OPP].start()
    c_z.start()
    g_y[FAR].forward()
    staged[2].wait()
    rows_a.scatter()
    rows_a.scatter_rest()
    h_x[NEAR].middle()
    g_y[OWN].start()
    g_y[OPP].forward()
    hidden(FAR)
    c_x[OWN].forward()
    g_y[OWN].forward()
    hidden(OPP)
    rows_a.near_ready()
    h_x[FAR].middle()
    hidden_end(NEAR)
    hidden(OWN)
    h_x[OPP].middle()
    a_y[NEAR].start()
    hidden_end(FAR)
    h_x[OWN].middle()
    hidden_end(OPP)
    weights(1, w_in, WI)
    hidden_end(OWN)
    c_z.here()
    c_x[NEAR].start()
    rows_a.far_ready()
    a_y[FAR].start()
    rows_a.opp_ready()
    a_y[NEAR].forward()
    a_y[OPP].start()
    c_x[OWN].done()
    weight_grad(1, OWN, True)
    c_x[FAR].start()
    rows_a.own_ready()
    dh_rows()
    d_x[OWN].start()
    d_z.start()
    a_y[FAR].forward()
    a_y[OWN].start()
    d_x[OWN].forward()
    a_y[OPP].forward()
    d_z.here()
    d_x[UP].start()
    d_z.send_on()
    inputs(OWN, True)
    a_y[OWN].forward()
    d_x[DOWN].start()
    c_z.send_on()
    d_x[UP].forward()
    d_z.done()
    d_x[OPP].start()
    q_y[OWN].middle()
    d_x[DOWN].forward()
    inputs(UP)
    inputs_end(OWN)
    d_x[OPP].forward()
    c_x[NEAR].forward()
    c_x[FAR].forward()
    c_z.done()
    c_x[OPP].start()
    inputs(DOWN)
    q_y[UP].middle()
    inputs_out(OWN)
    for t in range(4):
        a_y[t].done()
    weight_grad(0, OWN, True)
    weight_grad(0, UP)
    inputs(OPP)
    q_y[DOWN].middle()
    inputs_end(UP)
    weight_grad(0, DOWN)
    weight_grad(0, OPP)
    share(0)
    q_y[OPP].middle()
    inputs_end(DOWN)
    bias_sums()
    c_x[OPP].forward()
    c_x[NEAR].done()
    weight_grad(1, NEAR)
    inputs_end(OPP)
    inputs_out(UP)
    c_x[FAR].done()
    weight_grad(1, FAR)
    inputs_out(DOWN)
    c_x[OPP].done()
    weight_grad(1, OPP)
    share(1)
    inputs_out(OPP)
    finish_weight(0, o_iw)
    finish_bias()
    finish_weight(1, o_ow)
    finish_inputs()
    finish_sends()


def deliver(from_ig, from_iw, from_ow, from_bias, o_ig, o_iw, o_ow, o_bias, sem):
    pieces = [(from_bias, o_bias)]
    for src, dst, rows in ((from_iw, o_iw, 224), (from_ow, o_ow, 224), (from_ig, o_ig, 16)):
        for k in range(src.shape[0] // rows):
            at = pl.ds(k * rows, rows)
            pieces.append((src.at[at], dst.at[at]))
    copies = [pltpu.make_async_copy(a, b, sem.at[k]) for k, (a, b) in enumerate(pieces)]
    for copy in copies:
        copy.start()
    for copy in copies:
        copy.wait()


def shards(acts, preact, out_grad, w_in, w_out):
    vmem = pl.BlockSpec(memory_space=pltpu.VMEM)
    bf = lambda *shape: pltpu.VMEM(shape, BF)
    f32 = lambda *shape: pltpu.VMEM(shape, F32)
    scratch = dict(
        acts=bf(32, 4 * W), pre=bf(64, W), grad=bf(32, 4 * W),
        G=bf(4, 4, 64, W), A=bf(4, 4, 64, W), AC=bf(4, 4, 64, W), D=bf(4, 4, 64, W),
        WO=bf(W, W), WI=bf(W, W),
        HP=bf(4, 4, 64, W), H1=bf(4, 2, 32, W), H2=bf(4, 2, 64, W), HX=bf(4, 2, 32, W),
        HS=f32(64, W), HB=bf(3, 64, W), ZR=bf(3, 64, W), SL=f32(64, W),
        QP=bf(4, 4, 64, W), Q1=bf(4, 2, 32, W), Q2=bf(4, 2, 64, W), QX=bf(4, 2, 32, W),
        QS=f32(4, 64, W), ZS=bf(4, 32, W), ZL=bf(4, 32, W), IS=bf(4, 32, W), IR=bf(4, 32, W),
        ACC=f32(2, W, W), WS=bf(2, 448, W), WR=bf(2, 448, W),
        BS=f32(8, W), BR=f32(8, W),
        send_sem=pltpu.SemaphoreType.DMA((N_SENDS,)),
        recv_sem=pltpu.SemaphoreType.DMA((N_SEMS,)),
        local_sem=pltpu.SemaphoreType.DMA((16,)),
    )
    hbm = pl.BlockSpec(memory_space=pl.ANY)
    parts = pl.pallas_call(
        kernel,
        out_shape=(bf(32, 4 * W), bf(448, W), bf(448, W), f32(W)),
        in_specs=[hbm] * 5,
        out_specs=[vmem] * 4,
        scratch_shapes=list(scratch.values()),
        compiler_params=pltpu.CompilerParams(
            collective_id=0, has_side_effects=True, vmem_limit_bytes=60 * 2**20
        ),
    )(acts, preact, out_grad, w_in, w_out)
    return pl.pallas_call(
        deliver,
        out_shape=tuple(jax.ShapeDtypeStruct(p.shape, p.dtype) for p in parts),
        in_specs=[vmem] * 4,
        out_specs=[hbm] * 4,
        scratch_shapes=[pltpu.SemaphoreType.DMA((7,))],
        compiler_params=pltpu.CompilerParams(vmem_limit_bytes=2**20),
    )(*parts)


def solution(mesh):
    return jax.shard_map(
        shards,
        mesh=mesh,
        in_specs=(
            P(("gz", "gy"), "gx"),
            P(("gz", "gx"), "gy"),
            P(("gz", "gy"), "gx"),
            P(("gx", "gz"), "gy"),
            P(("gx", "gz"), "gy"),
        ),
        out_specs=(P(("gz", "gy"), "gx"), P(("gx", "gz"), "gy"), P(("gx", "gz"), "gy"), P("gy")),
        check_vma=False,
    )
```
